32 devices in a mesh: seg: 8 (over z, y), blk: 4 (over x, core).
Axes of the slice: x: 2, y: 2, z: 4, core: 2. Of those that a mesh axis runs over, the one named last changes fastest.
Arguments:
- queries: float32 [4096, 1024], P(('seg', 'blk')), may hold values from -5 to 5
- keys: float32 [4096, 256], P(('seg', 'blk')), may hold values from -5 to 5
- values: float32 [4096, 256], P(('seg', 'blk')), may hold values from -6 to 6
- gate_logit: float32 [8], replicated, may hold values from -3 to 3
- memory_gain: float32 [1024], replicated, may hold values from 0.5 to 2
Outputs:
- mixed: float32 [4096, 1024], P(('seg', 'blk'))
The draws below stay inside these ranges and needn't reach their ends.
All inputs are finite; a program needn't handle non-finite values.
Results may differ from the reference program's by a relative error of at most 0.0003.
Values sent between devices are 32-bit elements; how exact they have to be, the bound alone decides.
No kernel may reach another device: no remote copies, remote signals or barrier semaphores. Data moves between devices by JAX's collectives and lax.ppermute only.
A program may use at most 64 MiB of HBM per device.

```python
import math
import jax
import jax.numpy as jnp
from jax import lax

ROWS = 128
QH = 8
KVH = 2
GROUP = 4
HD = 128
SEQ = 4096
N_SEG = 8
N_BLK = 4


def draw_keys(key, part):
    base = jnp.clip(jax.random.normal(jax.random.fold_in(key, 11), (SEQ, KVH * HD), jnp.float32), -5.0, 5.0)
    return base


def draw_queries(key, part):
    base = jnp.clip(jax.random.normal(jax.random.fold_in(key, 13), (SEQ, QH * HD), jnp.float32), -5.0, 5.0)
    return base


def block_scale(own_key, shape, cuts, low, largest):
    level, own = 1.0, jax.random.fold_in(own_key, 6)
    for dim, shards_of in cuts:
        draws = jnp.exp(jax.random.uniform(jax.random.fold_in(own, dim), (shards_of,), jnp.float32, low / len(cuts), largest / len(cuts)))
        level = level * jnp.repeat(draws, shape[dim] // shards_of).reshape([-1 if axis == dim else 1 for axis in range(len(shape))])
    return level


def gaussian(key, extent, deviation, bound, shards=(), kind=jnp.bfloat16):
    level = block_scale(key, extent, shards, -0.22, 0.18) if shards else 1.0
    array = jax.random.normal(key, extent, jnp.float32) * deviation * level
    return jnp.minimum(jnp.maximum(array, -bound), bound).astype(kind)


def setup_inputs(seed: int = 0) -> dict:
    splits = jax.random.split(jax.random.key(seed), 6)
    queries = draw_queries(jax.random.fold_in(splits[5], 71), 0)
    keys = draw_keys(jax.random.fold_in(splits[5], 71), 0)
    values = gaussian(splits[2], (SEQ, KVH * HD), 1.0, 6.0, ((0, 32),), jnp.float32)
    gate_logit = jnp.clip(jax.random.uniform(splits[3], (QH,), jnp.float32, -3.0, 3.0), -3.0, 3.0)
    memory_gain = jnp.clip(jnp.exp(jax.random.uniform(splits[4], (QH * HD,), jnp.float32, math.log(0.5), math.log(2.0))), 0.5, 2.0)
    return dict(queries=queries, keys=keys, values=values, gate_logit=gate_logit, memory_gain=memory_gain)


HIGH = lax.Precision.HIGHEST

def sigma_map(x):
    return jnp.where(x > 0, x + 1.0, jnp.exp(jnp.minimum(x, 0.0)))

def segment_out(operands):
    q_seg, k_seg, v_seg, memory_seg = operands
    length = q_seg.shape[0]
    q_heads = q_seg.reshape(length, KVH, GROUP, HD)
    k_heads = k_seg.reshape(length, KVH, HD)
    v_heads = v_seg.reshape(length, KVH, HD)
    qpos = jnp.arange(length, dtype=jnp.int32)
    causal = qpos[None, :] <= qpos[:, None]

    def one_head(inputs):
        qh, kh, vh = inputs
        scores = jnp.einsum('rgd,nd->grn', qh, kh, precision=HIGH) / jnp.sqrt(jnp.float32(HD))
        scores = jnp.where(causal[None], scores, -1e+30)
        top = lax.optimization_barrier(jnp.max(scores, axis=-1, keepdims=True))
        weights = jnp.where(causal[None], jnp.exp(scores - top), 0.0)
        total = lax.optimization_barrier(jnp.sum(weights, axis=-1, keepdims=True))
        return jnp.einsum('grn,nd->grd', weights, vh, precision=HIGH) / total
    attention = lax.map(one_head, (jnp.transpose(q_heads, (1, 0, 2, 3)), jnp.transpose(k_heads, (1, 0, 2)), jnp.transpose(v_heads, (1, 0, 2))))
    retrieval = jnp.einsum('rkgd,kde->kgre', sigma_map(q_heads), memory_seg, precision=HIGH)
    return (attention, retrieval)

def reference(queries, keys, values, gate_logit, memory_gain):
    seg_count = N_SEG
    length = ROWS * N_BLK
    k_all = keys.reshape(seg_count, length, KVH, HD)
    v_all = values.reshape(seg_count, length, KVH, HD)
    partial_value = jnp.einsum('gskd,gske->gkde', sigma_map(k_all), v_all, precision=HIGH)
    memory = jnp.cumsum(partial_value, axis=0) - partial_value
    attention, retrieval = lax.map(segment_out, (queries.reshape(seg_count, length, QH * HD), keys.reshape(seg_count, length, KVH * HD), values.reshape(seg_count, length, KVH * HD), memory))
    rms = jnp.sqrt(lax.optimization_barrier(jnp.mean(retrieval * retrieval, axis=-1, keepdims=True)) + 1e-06)
    gain = memory_gain.reshape(KVH, GROUP, 1, HD)
    normed = retrieval / rms * gain
    gate = jax.nn.sigmoid(gate_logit).reshape(KVH, GROUP, 1, 1)
    mixed = gate * normed + (1.0 - gate) * attention
    return jnp.transpose(mixed, (0, 3, 1, 2, 4)).reshape(seg_count * length, QH * HD)
```

```python
import jax
import jax.numpy as jnp
from jax import lax
from jax.experimental import pallas as pl
from jax.experimental.pallas import tpu as pltpu
from jax.sharding import PartitionSpec as P

HD = 128
EPS = 1e-6
NEG = -1e30


def sigma_map(x):
    return jnp.where(x > 0, x + 1.0, jnp.exp(jnp.minimum(x, 0.0)))


def split(x):
    high = x.astype(jnp.bfloat16)
    low = (x - high.astype(jnp.float32)).astype(jnp.bfloat16)
    return high, low


def dot(a, b, dims):
    return lax.dot_general(a, b, (dims, ((), ())), preferred_element_type=jnp.float32)


def partial_kernel(k_ref, v_ref, kc_ref, vc_ref, p_ref):
    head = lax.axis_index("blk") & 1
    cols = pl.ds(pl.multiple_of(head * HD, HD), HD)
    s_hi, s_lo = split(sigma_map(jnp.concatenate([k_ref[:, cols], kc_ref[:, cols]], 0)))
    v_hi, v_lo = split(jnp.concatenate([v_ref[:, cols], vc_ref[:, cols]], 0))
    left = jnp.concatenate([s_hi, s_lo, s_hi], 0)
    right = jnp.concatenate([v_hi, v_hi, v_lo], 0)
    p_ref[...] = dot(left, right, ((0,), (0,)))


def attention_kernel(group, chunks, *refs):
    q_ref = refs[0]
    k_refs = refs[1 : 1 + chunks]
    v_refs = refs[1 + chunks : 1 + 2 * chunks]
    gate_ref, gain_ref = refs[1 + 2 * chunks : 3 + 2 * chunks]
    att_ref, sh_ref, sl_ref, mult_ref = refs[3 + 2 * chunks :]
    rows = q_ref.shape[0]
    kv_heads = k_refs[0].shape[1] // HD
    place = lax.axis_index("blk")
    gates = 1.0 / (1.0 + jnp.exp(-gate_ref[...]))
    causal = lax.broadcasted_iota(jnp.int32, (rows, rows), 1) <= lax.broadcasted_iota(
        jnp.int32, (rows, rows), 0
    )
    causal = jnp.concatenate([causal] * group, 0)
    scale = 1.0 / jnp.sqrt(jnp.float32(HD))
    for head in range(kv_heads):
        kv = slice(head * HD, (head + 1) * HD)
        spans = [
            slice((head * group + g) * HD, (head * group + g + 1) * HD) for g in range(group)
        ]
        q = jnp.concatenate([q_ref[:, s] for s in spans], 0)
        f_hi, f_lo = split(sigma_map(q))
        for g, s in enumerate(spans):
            sh_ref[:, s] = f_hi[g * rows : (g + 1) * rows]
            sl_ref[:, s] = f_lo[g * rows : (g + 1) * rows]
        q_hi, q_lo = split(q * scale)
        left = jnp.concatenate([q_hi, q_lo], 1)
        scores = []
        for m in range(chunks):
            k_hi, k_lo = split(k_refs[m][:, kv])
            piece = dot(left, jnp.concatenate([k_hi, k_hi], 1), ((1,), (1,)))
            piece = piece + dot(q_hi, k_lo, ((1,), (1,)))
            if m == 0:
                piece = jnp.where(causal, piece, NEG)
            else:
                piece = jnp.where((place ^ m) < place, piece, NEG)
            scores.append(piece)
        top = scores[0]
        for piece in scores[1:]:
            top = jnp.maximum(top, piece)
        top = jnp.max(top, axis=1, keepdims=True)
        accum = None
        summed = None
        for m in range(chunks):
            w = jnp.exp(scores[m] - top)
            v_hi, v_lo = split(v_refs[m][:, kv])
            w_hi, w_lo = split(w)
            both = dot(w_hi, jnp.concatenate([v_hi, v_lo], 1), ((1,), (0,)))
            part = both[:, :HD] + both[:, HD:] + dot(w_lo, v_hi, ((1,), (0,)))
            accum = part if accum is None else accum + part
            summed = w if summed is None else summed + w
        att = accum / jnp.sum(summed, axis=1, keepdims=True)
        for g, s in enumerate(spans):
            h = head * group + g
            gate = gates[:, h : h + 1]
            att_ref[:, s] = (1.0 - gate) * att[g * rows : (g + 1) * rows]
            mult_ref[:, s] = gate * gain_ref[:, s]


def final_kernel(group, att_ref, sh_ref, sl_ref, mult_ref, mine_ref, other_ref, out_ref):
    rows = att_ref.shape[0]
    kv_heads = att_ref.shape[1] // (group * HD)
    own = lax.axis_index("blk") & 1
    for head in range(kv_heads):
        memory = jnp.where(own == head, mine_ref[...], other_ref[...])
        m_hi, m_lo = split(memory)
        right = jnp.concatenate([m_hi, m_hi], 0)
        spans = [
            slice((head * group + g) * HD, (head * group + g + 1) * HD) for g in range(group)
        ]
        f_hi = jnp.concatenate([sh_ref[:, s] for s in spans], 0)
        f_lo = jnp.concatenate([sl_ref[:, s] for s in spans], 0)
        r = dot(jnp.concatenate([f_hi, f_lo], 1), right, ((1,), (0,)))
        r = r + dot(f_hi, m_lo, ((1,), (0,)))
        inv = lax.rsqrt(jnp.mean(r * r, axis=1, keepdims=True) + EPS)
        r = r * inv
        for g, s in enumerate(spans):
            out_ref[:, s] = att_ref[:, s] + r[g * rows : (g + 1) * rows] * mult_ref[:, s]


def solution(mesh):
    n_seg, n_blk = mesh.shape["seg"], mesh.shape["blk"]
    both = ("seg", "blk")

    def swap(x, seg_bits, blk_bits):
        pairs = [
            (s * n_blk + b, (s ^ seg_bits) * n_blk + (b ^ blk_bits))
            for s in range(n_seg)
            for b in range(n_blk)
        ]
        return lax.ppermute(x, both, pairs)

    bits = [(1 << i, 0) for i in reversed(range(n_seg.bit_length() - 1))]
    bits += [(0, 1 << i) for i in reversed(range(1, n_blk.bit_length() - 1))]
    stages = [bits[i : i + 2] for i in range(0, len(bits), 2)]

    def on_device(queries, keys, values, gate_logit, memory_gain):
        rows, width = queries.shape
        kv_width = keys.shape[1]
        group = width // kv_width
        seg = lax.axis_index("seg")

        k_held, v_held = [keys], [values]
        k_held.append(swap(keys, 0, 1))
        v_held.append(swap(values, 0, 1))
        part = pl.pallas_call(
            partial_kernel, out_shape=jax.ShapeDtypeStruct((HD, HD), jnp.float32)
        )(k_held[0], v_held[0], k_held[1], v_held[1])

        step = 2
        while step < n_blk:
            fresh_k = [swap(k_held[m], 0, step) for m in range(0, step, 2)]
            fresh_v = [swap(v_held[m], 0, step) for m in range(0, step, 2)]
            for k_new, v_new in zip(fresh_k, fresh_v, strict=True):
                k_held += [k_new, swap(k_new, 0, 1)]
                v_held += [v_new, swap(v_new, 0, 1)]
            step *= 2

        carried = None
        for stage in stages:
            masks = [(0, 0)]
            for s, b in stage:
                masks += [(s ^ p, b ^ q) for p, q in masks]
            total = carried
            for s, b in masks[1:]:
                if s:
                    sent = part if carried is None else carried + jnp.where((seg ^ s) > seg, part, 0.0)
                else:
                    sent = carried if carried is not None else jnp.zeros_like(part)
                got = swap(sent, s, b)
                if carried is None:
                    got = jnp.where((seg ^ s) < seg, got, 0.0)
                total = got if total is None else total + got
            carried = total
        mine = carried
        other = swap(mine, 0, 1)

        att, f_hi, f_lo, mult = pl.pallas_call(
            lambda *refs: attention_kernel(group, n_blk, *refs),
            out_shape=(
                jax.ShapeDtypeStruct((rows, width), jnp.float32),
                jax.ShapeDtypeStruct((rows, width), jnp.bfloat16),
                jax.ShapeDtypeStruct((rows, width), jnp.bfloat16),
                jax.ShapeDtypeStruct((1, width), jnp.float32),
            ),
            compiler_params=pltpu.CompilerParams(vmem_limit_bytes=48 * 1024 * 1024),
        )(
            queries,
            *k_held,
            *v_held,
            gate_logit.reshape(1, -1),
            memory_gain.reshape(1, -1),
        )
        return pl.pallas_call(
            lambda *refs: final_kernel(group, *refs),
            out_shape=jax.ShapeDtypeStruct((rows, width), jnp.float32),
            compiler_params=pltpu.CompilerParams(vmem_limit_bytes=48 * 1024 * 1024),
        )(att, f_hi, f_lo, mult, mine, other)

    return jax.shard_map(
        on_device,
        mesh=mesh,
        in_specs=(P(both, None), P(both, None), P(both, None), P(), P()),
        out_specs=P(both, None),
        check_vma=False,
    )
```

```python
import functools

import jax
import jax.numpy as jnp
from jax import lax
from jax.experimental import pallas as pl
from jax.experimental.pallas import tpu as pltpu
from jax.sharding import PartitionSpec as P

HD = 128
EPS = 1e-6
NEG = -1e30


def sigma_map(x):
    return jnp.where(x > 0, x + 1.0, jnp.exp(jnp.minimum(x, 0.0)))


def split(x):
    high = x.astype(jnp.bfloat16)
    low = (x - high.astype(jnp.float32)).astype(jnp.bfloat16)
    return high, low


def dot(a, b, dims):
    return lax.dot_general(a, b, (dims, ((), ())), preferred_element_type=jnp.float32)


def carried_head(lines):
    head = lax.axis_index("blk") & 1
    for axis, bit in lines:
        head = head ^ ((lax.axis_index(axis) >> bit) & 1)
    return head


def partial_kernel(lines, has_part, passed, *refs):
    k_ref, v_ref = refs[:2]
    out_ref = refs[2 + has_part + passed]
    head = carried_head(lines)
    cols = pl.ds(pl.multiple_of(head * HD, HD), HD)
    s_hi, s_lo = split(sigma_map(k_ref[:, cols]))
    v_hi, v_lo = split(v_ref[:, cols])
    left = jnp.concatenate([s_hi, s_lo, s_hi], 0)
    right = jnp.concatenate([v_hi, v_hi, v_lo], 0)
    part = dot(left, right, ((0,), (0,)))
    if has_part:
        out_ref[...] = refs[2][...] + part
    else:
        out_ref[...] = part
        refs[-2][...] = k_ref[...]
        refs[-1][...] = v_ref[...]


def combine_kernel(masks, nexts, carries, loose, *refs):
    count = len(masks)
    part_ref = refs[0]
    got_refs = refs[1 : 1 + count]
    outs = refs[1 + count + carries + loose :]
    seg = lax.axis_index("seg")
    total = refs[1 + count][...] if carries else None
    for (s, _), got_ref in zip(masks, got_refs, strict=True):
        got = got_ref[...]
        if not carries:
            got = jnp.where((seg ^ s) < seg, got, 0.0)
        total = got if total is None else total + got
    outs[0][...] = total
    for s, out_ref in zip(nexts, outs[1 : 1 + len(nexts)], strict=True):
        out_ref[...] = total + jnp.where((seg ^ s) > seg, part_ref[...], 0.0)


def attend(q_hi, q_lo, pieces, causal):
    left = jnp.concatenate([q_hi, q_lo], 1)
    scores = []
    for k, _ in pieces:
        k_hi, k_lo = split(k)
        piece = dot(left, jnp.concatenate([k_hi, k_hi], 1), ((1,), (1,)))
        scores.append(piece + dot(q_hi, k_lo, ((1,), (1,))))
    if causal is not None:
        scores[0] = jnp.where(causal, scores[0], NEG)
    top = functools.reduce(jnp.maximum, scores)
    top = jnp.max(top, axis=1, keepdims=True)
    accum, summed = [], []
    for piece, (_, v) in zip(scores, pieces, strict=True):
        w = jnp.exp(piece - top)
        v_hi, v_lo = split(v)
        w_hi, w_lo = split(w)
        both = dot(w_hi, jnp.concatenate([v_hi, v_lo], 1), ((1,), (0,)))
        accum.append(both[:, :HD] + both[:, HD:] + dot(w_lo, v_hi, ((1,), (0,))))
        summed.append(w)
    total = jnp.sum(functools.reduce(jnp.add, summed), axis=1, keepdims=True)
    return top, total, functools.reduce(jnp.add, accum)


def load_queries(q_ref, group, head):
    spans = [slice((head * group + g) * HD, (head * group + g + 1) * HD) for g in range(group)]
    return spans, jnp.concatenate([q_ref[:, s] for s in spans], 0)


def local_kernel(group, *refs):
    q_ref, k_ref, kc_ref, v_ref, vc_ref, gate_ref, gain_ref = refs[:7]
    acc_ref, top_ref, total_ref, sh_ref, sl_ref, mult_ref = refs[7:]
    rows = q_ref.shape[0]
    kv_heads = k_ref.shape[1] // HD
    second = (lax.axis_index("blk") & 1) == 1
    gates = 1.0 / (1.0 + jnp.exp(-gate_ref[...]))
    causal = lax.broadcasted_iota(jnp.int32, (rows, rows), 1) <= lax.broadcasted_iota(
        jnp.int32, (rows, rows), 0
    )
    causal = jnp.concatenate([causal] * group, 0)
    scale = 1.0 / jnp.sqrt(jnp.float32(HD))

    def work(with_other):
        for head in range(kv_heads):
            kv = slice(head * HD, (head + 1) * HD)
            spans, q = load_queries(q_ref, group, head)
            f_hi, f_lo = split(sigma_map(q))
            pieces = [(k_ref[:, kv], v_ref[:, kv])]
            if with_other:
                pieces.append((kc_ref[:, kv], vc_ref[:, kv]))
            top, total, accum = attend(*split(q * scale), pieces, causal)
            for g, s in enumerate(spans):
                h = head * group + g
                part = slice(g * rows, (g + 1) * rows)
                sh_ref[:, s] = f_hi[part]
                sl_ref[:, s] = f_lo[part]
                acc_ref[:, s] = accum[part]
                top_ref[:, h : h + 1] = top[part]
                total_ref[:, h : h + 1] = total[part]
                mult_ref[:, s] = gates[:, h : h + 1] * gain_ref[:, s]

    pl.when(second)(lambda: work(True))
    pl.when(jnp.logical_not(second))(lambda: work(False))


def remote_kernel(group, chunks, *refs):
    q_ref = refs[0]
    k_refs, v_refs = refs[1 : 1 + chunks], refs[1 + chunks : 1 + 2 * chunks]
    acc_ref, top_ref, total_ref, gate_ref = refs[1 + 2 * chunks : 5 + 2 * chunks]
    att_ref, top_out, total_out, done_ref = refs[5 + 2 * chunks :]
    rows = q_ref.shape[0]
    kv_heads = k_refs[0].shape[1] // HD
    place = lax.axis_index("blk")
    scale = 1.0 / jnp.sqrt(jnp.float32(HD))
    top_out[...] = top_ref[...]
    total_out[...] = total_ref[...]
    att_ref[...] = acc_ref[...]

    def add_chunks(first, last):
        for head in range(kv_heads):
            kv = slice(head * HD, (head + 1) * HD)
            spans, q = load_queries(q_ref, group, head)
            pieces = [(k_refs[m][:, kv], v_refs[m][:, kv]) for m in range(first, last)]
            top, total, accum = attend(*split(q * scale), pieces, None)
            for g, s in enumerate(spans):
                h = head * group + g
                part = slice(g * rows, (g + 1) * rows)
                old = top_out[:, h : h + 1]
                peak = jnp.maximum(old, top[part])
                before, after = jnp.exp(old - peak), jnp.exp(top[part] - peak)
                total_out[:, h : h + 1] = total_out[:, h : h + 1] * before + total[part] * after
                att_ref[:, s] = att_ref[:, s] * before + accum[part] * after
                top_out[:, h : h + 1] = peak

    bit = 1
    while (1 << bit) < chunks + 2:
        first = (1 << bit) - 2
        pl.when(((place >> bit) & 1) == 1)(
            functools.partial(add_chunks, first, first + (1 << bit))
        )
        bit += 1
    gates = 1.0 / (1.0 + jnp.exp(-gate_ref[...]))
    for h in range(kv_heads * group):
        s = slice(h * HD, (h + 1) * HD)
        weight = (1.0 - gates[:, h : h + 1]) / total_out[:, h : h + 1]
        att_ref[:, s] = att_ref[:, s] * weight
    done_ref[...] = jnp.zeros_like(done_ref)


def final_kernel(group, lines, att_ref, sh_ref, sl_ref, mult_ref, mine_ref, other_ref, out_ref):
    rows = att_ref.shape[0]
    kv_heads = att_ref.shape[1] // (group * HD)
    own = carried_head(lines)
    for head in range(kv_heads):
        memory = jnp.where(own == head, mine_ref[...], other_ref[...])
        m_hi, m_lo = split(memory)
        right = jnp.concatenate([m_hi, m_hi], 0)
        spans = [
            slice((head * group + g) * HD, (head * group + g + 1) * HD) for g in range(group)
        ]
        f_hi = jnp.concatenate([sh_ref[:, s] for s in spans], 0)
        f_lo = jnp.concatenate([sl_ref[:, s] for s in spans], 0)
        r = dot(jnp.concatenate([f_hi, f_lo], 1), right, ((1,), (0,)))
        r = r + dot(f_hi, m_lo, ((1,), (0,)))
        inv = lax.rsqrt(jnp.mean(r * r, axis=1, keepdims=True) + EPS)
        r = r * inv
        for g, s in enumerate(spans):
            out_ref[:, s] = att_ref[:, s] + r[g * rows : (g + 1) * rows] * mult_ref[:, s]


def solution(mesh):
    n_seg, n_blk = mesh.shape["seg"], mesh.shape["blk"]
    both = ("seg", "blk")

    def swap(x, seg_bits, blk_bits):
        pairs = [
            (s * n_blk + b, (s ^ seg_bits) * n_blk + (b ^ blk_bits))
            for s in range(n_seg)
            for b in range(n_blk)
        ]
        return lax.ppermute(x, both, pairs)

    bits = [("seg", i) for i in reversed(range(n_seg.bit_length() - 1))]
    bits += [("blk", i) for i in reversed(range(1, n_blk.bit_length() - 1))]
    groups = [bits[i : i + 2] for i in range(0, len(bits), 2)]
    lines = groups[-1]

    def masks_of(number):
        found = [(0, 0)]
        for axis, bit in reversed(groups[number]):
            flip = int(number == len(groups) - 1)
            step = (1 << bit, flip) if axis == "seg" else (0, (1 << bit) ^ flip)
            found += [(s ^ step[0], b ^ step[1]) for s, b in found]
        return [found[i] for i in ((1, 3, 2) if number == 0 and len(found) > 3 else range(1, len(found)))]

    def on_device(queries, keys, values, gate_logit, memory_gain):
        rows, width = queries.shape
        group = width // keys.shape[1]
        square = jax.ShapeDtypeStruct((HD, HD), jnp.float32)

        def pass_on(kernel, inputs, loose, passed, outs, flops):
            anywhere = pl.BlockSpec(memory_space=pl.ANY)
            count, n_out = len(inputs) + len(loose), len(outs)
            return pl.pallas_call(
                kernel,
                in_specs=[pl.BlockSpec()] * len(inputs) + [anywhere] * (len(loose) + len(passed)),
                out_specs=[pl.BlockSpec()] * n_out + [anywhere] * len(passed),
                out_shape=outs
                + [jax.ShapeDtypeStruct(x.shape, x.dtype) for x in passed],
                input_output_aliases={count + i: n_out + i for i in range(len(passed))},
                compiler_params=pltpu.CompilerParams(vmem_limit_bytes=8 * 1024 * 1024),
                cost_estimate=pl.CostEstimate(
                    flops=flops, bytes_accessed=500_000, transcendentals=20_000
                ),
            )(*inputs, *loose, *passed)

        k_core, v_core = swap(keys, 0, 1), swap(values, 0, 1)
        tall = jax.ShapeDtypeStruct(keys.shape, jnp.float32)
        part, k_own, v_own = pass_on(
            functools.partial(partial_kernel, lines, 0, 0),
            [keys, values],
            [],
            [],
            [square, tall, tall],
            500_000_000,
        )
        part, k_own, v_own = pass_on(
            functools.partial(partial_kernel, lines, 1, 2),
            [k_core, v_core, part],
            [],
            [k_own, v_own],
            [square],
            500_000_000,
        )
        gate, gain = gate_logit.reshape(1, -1), memory_gain.reshape(1, -1)
        wide = jax.ShapeDtypeStruct((rows, width), jnp.float32)
        wide_half = jax.ShapeDtypeStruct((rows, width), jnp.bfloat16)
        per_head = jax.ShapeDtypeStruct((rows, width // HD), jnp.float32)
        line = jax.ShapeDtypeStruct((1, width), jnp.float32)
        large = pltpu.CompilerParams(vmem_limit_bytes=24 * 1024 * 1024)
        cost = pl.CostEstimate(flops=1_000_000_000, bytes_accessed=2_000_000, transcendentals=400_000)
        accum, top, total, f_hi, f_lo, mult = pl.pallas_call(
            functools.partial(local_kernel, group),
            out_shape=(wide, per_head, per_head, wide_half, wide_half, line),
            compiler_params=large,
            cost_estimate=cost,
        )(queries, k_own, k_core, v_own, v_core, gate, gain)

        k_held, v_held = [k_own, k_core], [v_own, v_core]
        fresh = [swap(k_own, 0, 2), swap(v_own, 0, 2)] if n_blk > 2 else []

        att = None
        carried = None
        sends = {s: part for s, _ in masks_of(0)}
        for number in range(len(groups)):
            masks = masks_of(number)
            got = [swap(sends[s], s, b) for s, b in masks]
            last = number == len(groups) - 1
            nexts = [] if last else sorted({s for s, _ in masks_of(number + 1) if s})
            some = [] if carried is None else [carried]
            loose = [mult] if number == 0 else [done] if last else []
            passed = fresh if number == 0 else []
            carried, *extra = pass_on(
                functools.partial(combine_kernel, masks, nexts, len(some), len(loose) + len(passed)),
                [part, *got, *some],
                loose,
                passed,
                [square] * (1 + len(nexts)),
                100_000,
            )
            sends = {0: carried, **dict(zip(nexts, extra[: len(nexts)], strict=True))}
            if number == 0:
                fresh = extra[len(nexts) :]
                step = 2
                while step < n_blk:
                    if step == 2:
                        fresh_k, fresh_v = fresh[:1], fresh[1:]
                    else:
                        fresh_k = [swap(k_held[m], 0, step) for m in range(0, step, 2)]
                        fresh_v = [swap(v_held[m], 0, step) for m in range(0, step, 2)]
                    for k_new, v_new in zip(fresh_k, fresh_v, strict=True):
                        k_held += [k_new, swap(k_new, 0, 1)]
                        v_held += [v_new, swap(v_new, 0, 1)]
                    step *= 2
                att, _, _, done = pl.pallas_call(
                    functools.partial(remote_kernel, group, n_blk - 2),
                    out_shape=(wide, per_head, per_head, jax.ShapeDtypeStruct((8, HD), jnp.float32)),
                    compiler_params=large,
                    cost_estimate=cost,
                )(queries, *k_held[2:], *v_held[2:], accum, top, total, gate)
        other = swap(carried, 0, 1)

        return pl.pallas_call(
            functools.partial(final_kernel, group, lines),
            out_shape=jax.ShapeDtypeStruct((rows, width), jnp.float32),
            compiler_params=pltpu.CompilerParams(vmem_limit_bytes=16 * 1024 * 1024),
        )(att, f_hi, f_lo, mult, carried, other)

    return jax.shard_map(
        on_device,
        mesh=mesh,
        in_specs=(P(both, None), P(both, None), P(both, None), P(), P()),
        out_specs=P(both, None),
        check_vma=False,
    )
```

```python
import functools

import jax
import jax.numpy as jnp
from jax import lax
from jax.experimental import pallas as pl
from jax.experimental.pallas import tpu as pltpu
from jax.sharding import PartitionSpec as P

HD = 128
EPS = 1e-6
NEG = -1e30


def sigma_map(x):
    return jnp.where(x > 0, x + 1.0, jnp.exp(jnp.minimum(x, 0.0)))


def split(x):
    high = x.astype(jnp.bfloat16)
    low = (x - high.astype(jnp.float32)).astype(jnp.bfloat16)
    return high, low


def dot(a, b, dims):
    return lax.dot_general(a, b, (dims, ((), ())), preferred_element_type=jnp.float32)


def carried_head(lines):
    head = lax.axis_index("blk") & 1
    for axis, bit in lines:
        head = head ^ ((lax.axis_index(axis) >> bit) & 1)
    return head


def add_partial(head, k_ref, v_ref):
    cols = pl.ds(pl.multiple_of(head * HD, HD), HD)
    s_hi, s_lo = split(sigma_map(k_ref[:, cols]))
    v_hi, v_lo = split(v_ref[:, cols])
    left = jnp.concatenate([s_hi, s_lo, s_hi], 0)
    right = jnp.concatenate([v_hi, v_hi, v_lo], 0)
    return dot(left, right, ((0,), (0,)))


def chip_kernel(lines, kv_ref, kc_ref, vc_ref, part_ref):
    half = kc_ref.shape[1]
    head = carried_head(lines)
    own = add_partial(head, kv_ref.at[:, :half], kv_ref.at[:, half:])
    part_ref[...] = own + add_partial(head, kc_ref, vc_ref)


def hold_kernel(*refs):
    pass


def combine_kernel(masks, nexts, carries, loose, *refs):
    count = len(masks)
    part_ref = refs[0]
    got_refs = refs[1 : 1 + count]
    outs = refs[1 + count + carries + loose :]
    seg = lax.axis_index("seg")
    total = refs[1 + count][...] if carries else None
    for (s, _), got_ref in zip(masks, got_refs, strict=True):
        got = got_ref[...]
        if not carries:
            got = jnp.where((seg ^ s) < seg, got, 0.0)
        total = got if total is None else total + got
    outs[0][...] = total
    for s, out_ref in zip(nexts, outs[1 : 1 + len(nexts)], strict=True):
        out_ref[...] = total + jnp.where((seg ^ s) > seg, part_ref[...], 0.0)


def attend(q_hi, q_lo, keys, values, mask):
    k_hi, k_lo = split(jnp.concatenate(keys, 0))
    v_hi, v_lo = split(jnp.concatenate(values, 0))
    left = jnp.concatenate([q_hi, q_lo], 1)
    scores = dot(left, jnp.concatenate([k_hi, k_hi], 1), ((1,), (1,)))
    scores = scores + dot(q_hi, k_lo, ((1,), (1,)))
    scores = mask(scores)
    top = jnp.max(scores, axis=1, keepdims=True)
    w = jnp.exp(scores - top)
    total = jnp.sum(w, axis=1, keepdims=True)
    w_hi, w_lo = split(w)
    both = dot(w_hi, jnp.concatenate([v_hi, v_lo], 1), ((1,), (0,)))
    return top, total, both[:, :HD] + both[:, HD:] + dot(w_lo, v_hi, ((1,), (0,)))


def prepare_kernel(group, *refs):
    q_ref, gate_ref, gain_ref = refs[:3]
    qh_ref, ql_ref, sh_ref, sl_ref, mult_ref, keep_ref = refs[3:]
    scale = 1.0 / jnp.sqrt(jnp.float32(HD))
    gates = 1.0 / (1.0 + jnp.exp(-gate_ref[...]))
    for h in range(q_ref.shape[1] // HD):
        s = slice(h * HD, (h + 1) * HD)
        q = q_ref[:, s]
        qh_ref[:, s], ql_ref[:, s] = split(q * scale)
        sh_ref[:, s], sl_ref[:, s] = split(sigma_map(q))
        gate = jnp.broadcast_to(gates[:, h : h + 1], (1, HD))
        mult_ref[:, s] = gate * gain_ref[:, s]
        keep_ref[:, s] = 1.0 - gate


def attention_kernel(group, chunks, *refs):
    qh_ref, ql_ref = refs[:2]
    half = refs[2].shape[1]
    k_refs = [ref.at[:, :half] for ref in refs[4 : 3 + chunks]]
    v_refs = [ref.at[:, half:] for ref in refs[4 : 3 + chunks]]
    k_refs.insert(1, refs[2])
    v_refs.insert(1, refs[3])
    keep_ref, att_ref, done_ref = refs[3 + chunks :]
    rows = qh_ref.shape[0]
    kv_heads = half // HD
    place = lax.axis_index("blk")
    causal = lax.broadcasted_iota(jnp.int32, (rows, rows), 1) <= lax.broadcasted_iota(
        jnp.int32, (rows, rows), 0
    )
    causal = jnp.concatenate([causal] * group, 0)

    def work(count):
        def mask(scores):
            pieces = [jnp.where(causal, scores[:, :rows], NEG)]
            for m in range(1, count // 2):
                piece = scores[:, m * rows : (m + 1) * rows]
                pieces.append(jnp.where((place ^ m) < place, piece, NEG))
            if count > 1:
                pieces.append(scores[:, max(count // 2, 1) * rows :])
            return jnp.concatenate(pieces, 1) if count > 1 else pieces[0]

        for head in range(kv_heads):
            kv = slice(head * HD, (head + 1) * HD)
            spans = [
                slice((head * group + g) * HD, (head * group + g + 1) * HD) for g in range(group)
            ]
            q_hi = jnp.concatenate([qh_ref[:, s] for s in spans], 0)
            q_lo = jnp.concatenate([ql_ref[:, s] for s in spans], 0)
            keys = [k_refs[m][:, kv] for m in range(count)]
            values = [v_refs[m][:, kv] for m in range(count)]
            _, total, accum = attend(q_hi, q_lo, keys, values, mask)
            accum = accum / total
            for g, s in enumerate(spans):
                att_ref[:, s] = accum[g * rows : (g + 1) * rows] * keep_ref[:, s]

    count = 1
    while count <= chunks:
        low, high = count // 2, count
        pl.when((place >= low) & (place < high))(functools.partial(work, count))
        count *= 2
    done_ref[...] = jnp.zeros_like(done_ref)


def final_kernel(group, lines, att_ref, sh_ref, sl_ref, mult_ref, mine_ref, other_ref, out_ref):
    rows = att_ref.shape[0]
    kv_heads = att_ref.shape[1] // (group * HD)
    own = carried_head(lines)
    for head in range(kv_heads):
        memory = jnp.where(own == head, mine_ref[...], other_ref[...])
        m_hi, m_lo = split(memory)
        right = jnp.concatenate([m_hi, m_hi], 0)
        spans = [
            slice((head * group + g) * HD, (head * group + g + 1) * HD) for g in range(group)
        ]
        f_hi = jnp.concatenate([sh_ref[:, s] for s in spans], 0)
        f_lo = jnp.concatenate([sl_ref[:, s] for s in spans], 0)
        r = dot(jnp.concatenate([f_hi, f_lo], 1), right, ((1,), (0,)))
        r = r + dot(f_hi, m_lo, ((1,), (0,)))
        inv = lax.rsqrt(jnp.mean(r * r, axis=1, keepdims=True) + EPS)
        r = r * inv
        for g, s in enumerate(spans):
            out_ref[:, s] = att_ref[:, s] + r[g * rows : (g + 1) * rows] * mult_ref[:, s]


def solution(mesh):
    n_seg, n_blk = mesh.shape["seg"], mesh.shape["blk"]
    both = ("seg", "blk")

    def swap(x, seg_bits, blk_bits):
        pairs = [
            (s * n_blk + b, (s ^ seg_bits) * n_blk + (b ^ blk_bits))
            for s in range(n_seg)
            for b in range(n_blk)
        ]
        return lax.ppermute(x, both, pairs)

    bits = [("seg", i) for i in reversed(range(n_seg.bit_length() - 1))]
    bits += [("blk", i) for i in reversed(range(1, n_blk.bit_length() - 1))]
    groups = [bits[i : i + 2] for i in range(0, len(bits), 2)]
    lines = groups[-1]

    def masks_of(number):
        found = [(0, 0)]
        for axis, bit in reversed(groups[number]):
            flip = int(number == len(groups) - 1)
            step = (1 << bit, flip) if axis == "seg" else (0, (1 << bit) ^ flip)
            found += [(s ^ step[0], b ^ step[1]) for s, b in found]
        return [found[i] for i in ((1, 3, 2) if number == 0 and len(found) > 3 else range(1, len(found)))]

    def on_device(queries, keys, values, gate_logit, memory_gain):
        rows, width = queries.shape
        group = width // keys.shape[1]
        square = jax.ShapeDtypeStruct((HD, HD), jnp.float32)

        def pass_on(kernel, inputs, loose, passed, outs, flops):
            anywhere = pl.BlockSpec(memory_space=pl.ANY)
            count, n_out = len(inputs) + len(loose), len(outs)
            return pl.pallas_call(
                kernel,
                in_specs=[pl.BlockSpec()] * len(inputs) + [anywhere] * (len(loose) + len(passed)),
                out_specs=[pl.BlockSpec()] * n_out + [anywhere] * len(passed),
                out_shape=outs
                + [jax.ShapeDtypeStruct(x.shape, x.dtype) for x in passed],
                input_output_aliases={count + i: n_out + i for i in range(len(passed))},
                compiler_params=pltpu.CompilerParams(vmem_limit_bytes=8 * 1024 * 1024),
                cost_estimate=pl.CostEstimate(
                    flops=flops, bytes_accessed=500_000, transcendentals=20_000
                ),
            )(*inputs, *loose, *passed)

        k_core, v_core = swap(keys, 0, 1), swap(values, 0, 1)
        own = jnp.concatenate([keys, values], 1)
        (part,) = pass_on(
            functools.partial(chip_kernel, lines), [own, k_core, v_core], [], [], [square], 500_000_000
        )
        gate, gain = gate_logit.reshape(1, -1), memory_gain.reshape(1, -1)
        wide = jax.ShapeDtypeStruct((rows, width), jnp.float32)
        half = jax.ShapeDtypeStruct((rows, width), jnp.bfloat16)
        line = jax.ShapeDtypeStruct((1, width), jnp.float32)
        large = pltpu.CompilerParams(vmem_limit_bytes=24 * 1024 * 1024)
        q_hi, q_lo, f_hi, f_lo, mult, keep = pl.pallas_call(
            functools.partial(prepare_kernel, group),
            out_shape=(half, half, half, half, line, line),
            compiler_params=large,
            cost_estimate=pl.CostEstimate(
                flops=1_000_000, bytes_accessed=100_000, transcendentals=0
            ),
        )(queries, gate, gain)

        held = [own, None]
        fresh = [swap(own, 0, 2)] if n_blk > 2 else []

        carried = None
        sends = {s: part for s, _ in masks_of(0)}
        for number in range(len(groups)):
            masks = masks_of(number)
            got = [swap(sends[s], s, b) for s, b in masks]
            last = number == len(groups) - 1
            nexts = [] if last else sorted({s for s, _ in masks_of(number + 1) if s})
            some = [] if carried is None else [carried]
            loose = [mult] if number == 0 else [done] if last else []
            carried, *extra = pass_on(
                functools.partial(combine_kernel, masks, nexts, len(some), len(loose)),
                [part, *got, *some],
                loose,
                [],
                [square] * (1 + len(nexts)),
                10_000_000_000 if number == 0 else 100_000,
            )
            sends = {0: carried, **dict(zip(nexts, extra, strict=True))}
            if number == 0:
                step = 2
                while step < n_blk:
                    if step == 2:
                        news = pass_on(hold_kernel, [], [carried], fresh, [], 0)
                    else:
                        news = [swap(held[m], 0, step) for m in range(0, step, 2)]
                    for new in news:
                        held += [new, swap(new, 0, 1)]
                    step *= 2
                att, done = pl.pallas_call(
                    functools.partial(attention_kernel, group, n_blk),
                    out_shape=(wide, jax.ShapeDtypeStruct((8, HD), jnp.float32)),
                    compiler_params=large,
                    cost_estimate=pl.CostEstimate(
                        flops=1_000_000, bytes_accessed=100_000, transcendentals=0
                    ),
                )(q_hi, q_lo, k_core, v_core, own, *held[2:], keep)
        other = swap(carried, 0, 1)

        return pl.pallas_call(
            functools.partial(final_kernel, group, lines),
            out_shape=jax.ShapeDtypeStruct((rows, width), jnp.float32),
            compiler_params=pltpu.CompilerParams(vmem_limit_bytes=16 * 1024 * 1024),
        )(att, f_hi, f_lo, mult, carried, other)

    return jax.shard_map(
        on_device,
        mesh=mesh,
        in_specs=(P(both, None), P(both, None), P(both, None), P(), P()),
        out_specs=P(both, None),
        check_vma=False,
    )
```

```python
import functools

import jax
import jax.numpy as jnp
from jax import lax
from jax.experimental import pallas as pl
from jax.experimental.pallas import tpu as pltpu
from jax.sharding import PartitionSpec as P

HD = 128
EPS = 1e-6
NEG = -1e30


def sigma_map(x):
    return jnp.where(x > 0, x + 1.0, jnp.exp(jnp.minimum(x, 0.0)))


def split(x):
    high = x.astype(jnp.bfloat16)
    low = (x - high.astype(jnp.float32)).astype(jnp.bfloat16)
    return high, low


def dot(a, b, dims):
    return lax.dot_general(a, b, (dims, ((), ())), preferred_element_type=jnp.float32)


def carried_head(lines):
    head = lax.axis_index("blk") & 1
    for axis, bit in lines:
        head = head ^ ((lax.axis_index(axis) >> bit) & 1)
    return head


def add_partial(head, k_ref, v_ref):
    cols = pl.ds(pl.multiple_of(head * HD, HD), HD)
    s_hi, s_lo = split(sigma_map(k_ref[:, cols]))
    v_hi, v_lo = split(v_ref[:, cols])
    left = jnp.concatenate([s_hi, s_lo, s_hi], 0)
    right = jnp.concatenate([v_hi, v_hi, v_lo], 0)
    return dot(left, right, ((0,), (0,)))


def chip_kernel(lines, kc_ref, vc_ref, kv_ref, part_ref, _):
    half = kc_ref.shape[1]
    head = carried_head(lines)
    own = add_partial(head, kv_ref.at[:, :half], kv_ref.at[:, half:])
    part_ref[...] = own + add_partial(head, kc_ref, vc_ref)


def combine_kernel(masks, nexts, carries, loose, *refs):
    count = len(masks)
    part_ref = refs[0]
    got_refs = refs[1 : 1 + count]
    outs = refs[1 + count + carries + loose :]
    seg = lax.axis_index("seg")
    total = refs[1 + count][...] if carries else None
    for (s, _), got_ref in zip(masks, got_refs, strict=True):
        got = got_ref[...]
        if not carries:
            got = jnp.where((seg ^ s) < seg, got, 0.0)
        total = got if total is None else total + got
    outs[0][...] = total
    for s, out_ref in zip(nexts, outs[1 : 1 + len(nexts)], strict=True):
        out_ref[...] = total + jnp.where((seg ^ s) > seg, part_ref[...], 0.0)


def attend(q_hi, q_lo, keys, values, mask):
    k_hi, k_lo = split(jnp.concatenate(keys, 0))
    v_hi, v_lo = split(jnp.concatenate(values, 0))
    left = jnp.concatenate([q_hi, q_lo], 1)
    scores = dot(left, jnp.concatenate([k_hi, k_hi], 1), ((1,), (1,)))
    scores = scores + dot(q_hi, k_lo, ((1,), (1,)))
    scores = mask(scores)
    top = jnp.max(scores, axis=1, keepdims=True)
    w = jnp.exp(scores - top)
    total = jnp.sum(w, axis=1, keepdims=True)
    w_hi, w_lo = split(w)
    both = dot(w_hi, jnp.concatenate([v_hi, v_lo], 1), ((1,), (0,)))
    return top, total, both[:, :HD] + both[:, HD:] + dot(w_lo, v_hi, ((1,), (0,)))


def prepare_kernel(group, *refs):
    q_ref, gate_ref, gain_ref = refs[:3]
    qh_ref, ql_ref, sh_ref, sl_ref, mult_ref, keep_ref = refs[3:]
    scale = 1.0 / jnp.sqrt(jnp.float32(HD))
    gates = 1.0 / (1.0 + jnp.exp(-gate_ref[...]))
    for h in range(q_ref.shape[1] // HD):
        s = slice(h * HD, (h + 1) * HD)
        q = q_ref[:, s]
        qh_ref[:, s], ql_ref[:, s] = split(q * scale)
        sh_ref[:, s], sl_ref[:, s] = split(sigma_map(q))
        gate = jnp.broadcast_to(gates[:, h : h + 1], (1, HD))
        mult_ref[:, s] = gate * gain_ref[:, s]
        keep_ref[:, s] = 1.0 - gate


def attention_kernel(group, chunks, *refs):
    qh_ref, ql_ref = refs[:2]
    half = refs[2].shape[1]
    k_refs = [ref.at[:, :half] for ref in refs[4 : 3 + chunks]]
    v_refs = [ref.at[:, half:] for ref in refs[4 : 3 + chunks]]
    k_refs.insert(1, refs[2])
    v_refs.insert(1, refs[3])
    keep_ref, att_ref, done_ref = refs[3 + chunks :]
    rows = qh_ref.shape[0]
    kv_heads = half // HD
    place = lax.axis_index("blk")
    causal = lax.broadcasted_iota(jnp.int32, (rows, rows), 1) <= lax.broadcasted_iota(
        jnp.int32, (rows, rows), 0
    )
    causal = jnp.concatenate([causal] * group, 0)

    def work(count):
        def mask(scores):
            pieces = [jnp.where(causal, scores[:, :rows], NEG)]
            for m in range(1, count // 2):
                piece = scores[:, m * rows : (m + 1) * rows]
                pieces.append(jnp.where((place ^ m) < place, piece, NEG))
            if count > 1:
                pieces.append(scores[:, max(count // 2, 1) * rows :])
            return jnp.concatenate(pieces, 1) if count > 1 else pieces[0]

        for head in range(kv_heads):
            kv = slice(head * HD, (head + 1) * HD)
            spans = [
                slice((head * group + g) * HD, (head * group + g + 1) * HD) for g in range(group)
            ]
            q_hi = jnp.concatenate([qh_ref[:, s] for s in spans], 0)
            q_lo = jnp.concatenate([ql_ref[:, s] for s in spans], 0)
            keys = [k_refs[m][:, kv] for m in range(count)]
            values = [v_refs[m][:, kv] for m in range(count)]
            _, total, accum = attend(q_hi, q_lo, keys, values, mask)
            accum = accum / total
            for g, s in enumerate(spans):
                att_ref[:, s] = accum[g * rows : (g + 1) * rows] * keep_ref[:, s]

    count = 1
    while count <= chunks:
        low, high = count // 2, count
        pl.when((place >= low) & (place < high))(functools.partial(work, count))
        count *= 2
    done_ref[...] = jnp.zeros_like(done_ref)


def final_kernel(group, lines, att_ref, sh_ref, sl_ref, mult_ref, mine_ref, other_ref, out_ref):
    rows = att_ref.shape[0]
    kv_heads = att_ref.shape[1] // (group * HD)
    own = carried_head(lines)
    for head in range(kv_heads):
        memory = jnp.where(own == head, mine_ref[...], other_ref[...])
        m_hi, m_lo = split(memory)
        right = jnp.concatenate([m_hi, m_hi], 0)
        spans = [
            slice((head * group + g) * HD, (head * group + g + 1) * HD) for g in range(group)
        ]
        f_hi = jnp.concatenate([sh_ref[:, s] for s in spans], 0)
        f_lo = jnp.concatenate([sl_ref[:, s] for s in spans], 0)
        r = dot(jnp.concatenate([f_hi, f_lo], 1), right, ((1,), (0,)))
        r = r + dot(f_hi, m_lo, ((1,), (0,)))
        inv = lax.rsqrt(jnp.mean(r * r, axis=1, keepdims=True) + EPS)
        r = r * inv
        for g, s in enumerate(spans):
            out_ref[:, s] = att_ref[:, s] + r[g * rows : (g + 1) * rows] * mult_ref[:, s]


def solution(mesh):
    n_seg, n_blk = mesh.shape["seg"], mesh.shape["blk"]
    both = ("seg", "blk")

    def swap(x, seg_bits, blk_bits):
        pairs = [
            (s * n_blk + b, (s ^ seg_bits) * n_blk + (b ^ blk_bits))
            for s in range(n_seg)
            for b in range(n_blk)
        ]
        return lax.ppermute(x, both, pairs)

    bits = [("seg", i) for i in reversed(range(n_seg.bit_length() - 1))]
    bits += [("blk", i) for i in reversed(range(1, n_blk.bit_length() - 1))]
    groups = [bits[i : i + 2] for i in range(0, len(bits), 2)]
    lines = groups[-1]

    def masks_of(number):
        found = [(0, 0)]
        for axis, bit in reversed(groups[number]):
            flip = int(number == len(groups) - 1)
            step = (1 << bit, flip) if axis == "seg" else (0, (1 << bit) ^ flip)
            found += [(s ^ step[0], b ^ step[1]) for s, b in found]
        return [found[i] for i in ((2, 3, 1) if number == 0 and len(found) > 3 else range(1, len(found)))]

    def on_device(queries, keys, values, gate_logit, memory_gain):
        rows, width = queries.shape
        group = width // keys.shape[1]
        square = jax.ShapeDtypeStruct((HD, HD), jnp.float32)

        def pass_on(kernel, inputs, loose, passed, outs, flops, passing=pl.BlockSpec(memory_space=pl.ANY)):
            anywhere = pl.BlockSpec(memory_space=pl.ANY)
            count, n_out = len(inputs) + len(loose), len(outs)
            return pl.pallas_call(
                kernel,
                in_specs=[pl.BlockSpec()] * len(inputs) + [anywhere] * len(loose) + [passing] * len(passed),
                out_specs=[pl.BlockSpec()] * n_out + [passing] * len(passed),
                out_shape=outs
                + [jax.ShapeDtypeStruct(x.shape, x.dtype) for x in passed],
                input_output_aliases={count + i: n_out + i for i in range(len(passed))},
                compiler_params=pltpu.CompilerParams(vmem_limit_bytes=8 * 1024 * 1024),
                cost_estimate=pl.CostEstimate(
                    flops=flops, bytes_accessed=500_000, transcendentals=20_000
                ),
            )(*inputs, *loose, *passed)

        k_core, v_core = swap(keys, 0, 1), swap(values, 0, 1)
        own = jnp.concatenate([keys, values], 1)
        part, own = pass_on(
            functools.partial(chip_kernel, lines), [k_core, v_core], [], [own], [square], 500_000_000, pl.BlockSpec()
        )
        gate, gain = gate_logit.reshape(1, -1), memory_gain.reshape(1, -1)
        wide = jax.ShapeDtypeStruct((rows, width), jnp.float32)
        half = jax.ShapeDtypeStruct((rows, width), jnp.bfloat16)
        line = jax.ShapeDtypeStruct((1, width), jnp.float32)
        large = pltpu.CompilerParams(vmem_limit_bytes=24 * 1024 * 1024)
        q_hi, q_lo, f_hi, f_lo, mult, keep = pl.pallas_call(
            functools.partial(prepare_kernel, group),
            out_shape=(half, half, half, half, line, line),
            compiler_params=large,
            cost_estimate=pl.CostEstimate(
                flops=1_000_000, bytes_accessed=100_000, transcendentals=0
            ),
        )(queries, gate, gain)

        held = [own, None]
        fresh = [swap(own, 0, 2)] if n_blk > 2 else []

        carried = None
        sends = {s: part for s, _ in masks_of(0)}
        for number in range(len(groups)):
            masks = masks_of(number)
            got = [swap(sends[s], s, b) for s, b in masks]
            last = number == len(groups) - 1
            nexts = [] if last else sorted({s for s, _ in masks_of(number + 1) if s})
            some = [] if carried is None else [carried]
            loose = [mult] if number == 0 else [done] if last else []
            carried, *extra = pass_on(
                functools.partial(combine_kernel, masks, nexts, len(some), len(loose)),
                [part, *got, *some],
                loose,
                [],
                [square] * (1 + len(nexts)),
                10_000_000_000 if number == 0 else 100_000,
            )
            sends = {0: carried, **dict(zip(nexts, extra, strict=True))}
            if number == 0:
                step = 2
                while step < n_blk:
                    news = fresh if step == 2 else [swap(held[m], 0, step) for m in range(0, step, 2)]
                    for new in news:
                        held += [new, swap(new, 0, 1)]
                    step *= 2
                att, done = pl.pallas_call(
                    functools.partial(attention_kernel, group, n_blk),
                    out_shape=(wide, jax.ShapeDtypeStruct((8, HD), jnp.float32)),
                    compiler_params=large,
                    cost_estimate=pl.CostEstimate(
                        flops=1_000_000, bytes_accessed=100_000, transcendentals=0
                    ),
                )(q_hi, q_lo, k_core, v_core, own, *held[2:], keep)
        other = swap(carried, 0, 1)

        return pl.pallas_call(
            functools.partial(final_kernel, group, lines),
            out_shape=jax.ShapeDtypeStruct((rows, width), jnp.float32),
            compiler_params=pltpu.CompilerParams(vmem_limit_bytes=16 * 1024 * 1024),
        )(att, f_hi, f_lo, mult, carried, other)

    return jax.shard_map(
        on_device,
        mesh=mesh,
        in_specs=(P(both, None), P(both, None), P(both, None), P(), P()),
        out_specs=P(both, None),
        check_vma=False,
    )
```

```python
import functools

import jax
import jax.numpy as jnp
from jax import lax
from jax.experimental import pallas as pl
from jax.experimental.pallas import tpu as pltpu
from jax.sharding import PartitionSpec as P

HD = 128
EPS = 1e-6
NEG = -1e30


def sigma_map(x):
    return jnp.where(x > 0, x + 1.0, jnp.exp(jnp.minimum(x, 0.0)))


def split(x):
    high = x.astype(jnp.bfloat16)
    low = (x - high.astype(jnp.float32)).astype(jnp.bfloat16)
    return high, low


def dot(a, b, dims):
    return lax.dot_general(a, b, (dims, ((), ())), preferred_element_type=jnp.float32)


def carried_head(lines):
    head = lax.axis_index("blk") & 1
    for axis, bit in lines:
        head = head ^ ((lax.axis_index(axis) >> bit) & 1)
    return head


def add_partial(head, k_ref, v_ref):
    cols = pl.ds(pl.multiple_of(head * HD, HD), HD)
    s_hi, s_lo = split(sigma_map(k_ref[:, cols]))
    v_hi, v_lo = split(v_ref[:, cols])
    left = jnp.concatenate([s_hi, s_lo, s_hi], 0)
    right = jnp.concatenate([v_hi, v_hi, v_lo], 0)
    return dot(left, right, ((0,), (0,)))


def chip_kernel(lines, kc_ref, vc_ref, kv_ref, part_ref, _):
    half = kc_ref.shape[1]
    head = carried_head(lines)
    own = add_partial(head, kv_ref.at[:, :half], kv_ref.at[:, half:])
    part_ref[...] = own + add_partial(head, kc_ref, vc_ref)


def combine_kernel(masks, nexts, carries, loose, *refs):
    count = len(masks)
    part_ref = refs[0]
    got_refs = refs[1 : 1 + count]
    outs = refs[1 + count + carries + loose :]
    seg = lax.axis_index("seg")
    total = refs[1 + count][...] if carries else None
    for (s, _), got_ref in zip(masks, got_refs, strict=True):
        got = got_ref[...]
        if not carries:
            got = jnp.where((seg ^ s) < seg, got, 0.0)
        total = got if total is None else total + got
    outs[0][...] = total
    for s, out_ref in zip(nexts, outs[1 : 1 + len(nexts)], strict=True):
        out_ref[...] = total + jnp.where((seg ^ s) > seg, part_ref[...], 0.0)


def attend(q_hi, q_lo, keys, values, mask):
    k_hi, k_lo = split(jnp.concatenate(keys, 0))
    v_hi, v_lo = split(jnp.concatenate(values, 0))
    left = jnp.concatenate([q_hi, q_lo], 1)
    scores = dot(left, jnp.concatenate([k_hi, k_hi], 1), ((1,), (1,)))
    scores = scores + dot(q_hi, k_lo, ((1,), (1,)))
    scores = mask(scores)
    top = jnp.max(scores, axis=1, keepdims=True)
    w = jnp.exp(scores - top)
    total = jnp.sum(w, axis=1, keepdims=True)
    w_hi, w_lo = split(w)
    both = dot(w_hi, jnp.concatenate([v_hi, v_lo], 1), ((1,), (0,)))
    return top, total, both[:, :HD] + both[:, HD:] + dot(w_lo, v_hi, ((1,), (0,)))


def prepare_kernel(group, *refs):
    q_ref, gate_ref, gain_ref = refs[:3]
    qh_ref, ql_ref, sh_ref, sl_ref, mult_ref, keep_ref = refs[3:]
    scale = 1.0 / jnp.sqrt(jnp.float32(HD))
    gates = 1.0 / (1.0 + jnp.exp(-gate_ref[...]))
    for h in range(q_ref.shape[1] // HD):
        s = slice(h * HD, (h + 1) * HD)
        q = q_ref[:, s]
        qh_ref[:, s], ql_ref[:, s] = split(q * scale)
        sh_ref[:, s], sl_ref[:, s] = split(sigma_map(q))
        gate = jnp.broadcast_to(gates[:, h : h + 1], (1, HD))
        mult_ref[:, s] = gate * gain_ref[:, s]
        keep_ref[:, s] = 1.0 - gate


def attention_kernel(group, chunks, *refs):
    qh_ref, ql_ref = refs[:2]
    half = refs[2].shape[1]
    k_refs = [ref.at[:, :half] for ref in refs[4 : 3 + chunks]]
    v_refs = [ref.at[:, half:] for ref in refs[4 : 3 + chunks]]
    k_refs.insert(1, refs[2])
    v_refs.insert(1, refs[3])
    keep_ref, att_ref, done_ref = refs[3 + chunks :]
    rows = qh_ref.shape[0]
    kv_heads = half // HD
    place = lax.axis_index("blk")
    causal = lax.broadcasted_iota(jnp.int32, (rows, rows), 1) <= lax.broadcasted_iota(
        jnp.int32, (rows, rows), 0
    )
    causal = jnp.concatenate([causal] * group, 0)

    def work(count):
        def mask(scores):
            pieces = [jnp.where(causal, scores[:, :rows], NEG)]
            for m in range(1, count // 2):
                piece = scores[:, m * rows : (m + 1) * rows]
                pieces.append(jnp.where((place ^ m) < place, piece, NEG))
            if count > 1:
                pieces.append(scores[:, max(count // 2, 1) * rows :])
            return jnp.concatenate(pieces, 1) if count > 1 else pieces[0]

        for head in range(kv_heads):
            kv = slice(head * HD, (head + 1) * HD)
            spans = [
                slice((head * group + g) * HD, (head * group + g + 1) * HD) for g in range(group)
            ]
            q_hi = jnp.concatenate([qh_ref[:, s] for s in spans], 0)
            q_lo = jnp.concatenate([ql_ref[:, s] for s in spans], 0)
            keys = [k_refs[m][:, kv] for m in range(count)]
            values = [v_refs[m][:, kv] for m in range(count)]
            _, total, accum = attend(q_hi, q_lo, keys, values, mask)
            accum = accum / total
            for g, s in enumerate(spans):
                att_ref[:, s] = accum[g * rows : (g + 1) * rows] * keep_ref[:, s]

    count = 1
    while count <= chunks:
        low, high = count // 2, count
        pl.when((place >= low) & (place < high))(functools.partial(work, count))
        count *= 2
    done_ref[...] = jnp.zeros_like(done_ref)


def final_kernel(group, lines, att_ref, sh_ref, sl_ref, mult_ref, mine_ref, other_ref, out_ref):
    rows = att_ref.shape[0]
    kv_heads = att_ref.shape[1] // (group * HD)
    own = carried_head(lines)
    for head in range(kv_heads):
        memory = jnp.where(own == head, mine_ref[...], other_ref[...])
        m_hi, m_lo = split(memory)
        right = jnp.concatenate([m_hi, m_hi], 0)
        spans = [
            slice((head * group + g) * HD, (head * group + g + 1) * HD) for g in range(group)
        ]
        f_hi = jnp.concatenate([sh_ref[:, s] for s in spans], 0)
        f_lo = jnp.concatenate([sl_ref[:, s] for s in spans], 0)
        r = dot(jnp.concatenate([f_hi, f_lo], 1), right, ((1,), (0,)))
        r = r + dot(f_hi, m_lo, ((1,), (0,)))
        inv = lax.rsqrt(jnp.mean(r * r, axis=1, keepdims=True) + EPS)
        r = r * inv
        for g, s in enumerate(spans):
            out_ref[:, s] = att_ref[:, s] + r[g * rows : (g + 1) * rows] * mult_ref[:, s]


def solution(mesh):
    n_seg, n_blk = mesh.shape["seg"], mesh.shape["blk"]
    both = ("seg", "blk")

    def swap(x, seg_bits, blk_bits):
        pairs = [
            (s * n_blk + b, (s ^ seg_bits) * n_blk + (b ^ blk_bits))
            for s in range(n_seg)
            for b in range(n_blk)
        ]
        return lax.ppermute(x, both, pairs)

    bits = [("seg", i) for i in reversed(range(n_seg.bit_length() - 1))]
    bits += [("blk", i) for i in reversed(range(1, n_blk.bit_length() - 1))]
    groups = [bits[i : i + 2] for i in range(0, len(bits), 2)]
    lines = groups[-1]

    def masks_of(number):
        found = [(0, 0)]
        for axis, bit in reversed(groups[number]):
            flip = int(number == len(groups) - 1)
            step = (1 << bit, flip) if axis == "seg" else (0, (1 << bit) ^ flip)
            found += [(s ^ step[0], b ^ step[1]) for s, b in found]
        return [found[i] for i in ((2, 3, 1) if number == 0 and len(found) > 3 else (3, 2, 1) if len(found) == 4 else range(1, len(found)))]

    def on_device(queries, keys, values, gate_logit, memory_gain):
        rows, width = queries.shape
        group = width // keys.shape[1]
        square = jax.ShapeDtypeStruct((HD, HD), jnp.float32)

        def pass_on(kernel, inputs, loose, passed, outs, flops, passing=pl.BlockSpec(memory_space=pl.ANY)):
            anywhere = pl.BlockSpec(memory_space=pl.ANY)
            count, n_out = len(inputs) + len(loose), len(outs)
            return pl.pallas_call(
                kernel,
                in_specs=[pl.BlockSpec()] * len(inputs) + [anywhere] * len(loose) + [passing] * len(passed),
                out_specs=[pl.BlockSpec()] * n_out + [passing] * len(passed),
                out_shape=outs
                + [jax.ShapeDtypeStruct(x.shape, x.dtype) for x in passed],
                input_output_aliases={count + i: n_out + i for i in range(len(passed))},
                compiler_params=pltpu.CompilerParams(vmem_limit_bytes=8 * 1024 * 1024),
                cost_estimate=pl.CostEstimate(
                    flops=flops, bytes_accessed=500_000, transcendentals=20_000
                ),
            )(*inputs, *loose, *passed)

        k_core, v_core = swap(keys, 0, 1), swap(values, 0, 1)
        own = jnp.concatenate([keys, values], 1)
        part, own = pass_on(
            functools.partial(chip_kernel, lines), [k_core, v_core], [], [own], [square], 500_000_000, pl.BlockSpec()
        )
        gate, gain = gate_logit.reshape(1, -1), memory_gain.reshape(1, -1)
        wide = jax.ShapeDtypeStruct((rows, width), jnp.float32)
        half = jax.ShapeDtypeStruct((rows, width), jnp.bfloat16)
        line = jax.ShapeDtypeStruct((1, width), jnp.float32)
        large = pltpu.CompilerParams(vmem_limit_bytes=24 * 1024 * 1024)
        q_hi, q_lo, f_hi, f_lo, mult, keep = pl.pallas_call(
            functools.partial(prepare_kernel, group),
            out_shape=(half, half, half, half, line, line),
            compiler_params=large,
            cost_estimate=pl.CostEstimate(
                flops=1_000_000, bytes_accessed=100_000, transcendentals=0
            ),
        )(queries, gate, gain)

        held = [own, None]
        fresh = [swap(own, 0, 2)] if n_blk > 2 else []

        carried = None
        sends = {s: part for s, _ in masks_of(0)}
        for number in range(len(groups)):
            masks = masks_of(number)
            got = [swap(sends[s], s, b) for s, b in masks]
            last = number == len(groups) - 1
            nexts = [] if last else sorted({s for s, _ in masks_of(number + 1) if s})
            some = [] if carried is None else [carried]
            loose = [mult] if number == 0 else [done] if last else []
            carried, *extra = pass_on(
                functools.partial(combine_kernel, masks, nexts, len(some), len(loose)),
                [part, *got, *some],
                loose,
                [],
                [square] * (1 + len(nexts)),
                10_000_000_000 if number == 0 else 100_000,
            )
            sends = {0: carried, **dict(zip(nexts, extra, strict=True))}
            if number == 0:
                step = 2
                while step < n_blk:
                    news = fresh if step == 2 else [swap(held[m], 0, step) for m in range(0, step, 2)]
                    for new in news:
                        held += [new, swap(new, 0, 1)]
                    step *= 2
                att, done = pl.pallas_call(
                    functools.partial(attention_kernel, group, n_blk),
                    out_shape=(wide, jax.ShapeDtypeStruct((8, HD), jnp.float32)),
                    compiler_params=large,
                    cost_estimate=pl.CostEstimate(
                        flops=1_000_000, bytes_accessed=100_000, transcendentals=0
                    ),
                )(q_hi, q_lo, k_core, v_core, own, *held[2:], keep)
        other = swap(carried, 0, 1)

        return pl.pallas_call(
            functools.partial(final_kernel, group, lines),
            out_shape=jax.ShapeDtypeStruct((rows, width), jnp.float32),
            compiler_params=pltpu.CompilerParams(vmem_limit_bytes=16 * 1024 * 1024),
        )(att, f_hi, f_lo, mult, carried, other)

    return jax.shard_map(
        on_device,
        mesh=mesh,
        in_specs=(P(both, None), P(both, None), P(both, None), P(), P()),
        out_specs=P(both, None),
        check_vma=False,
    )
```

```python
import functools

import jax
import jax.numpy as jnp
from jax import lax
from jax.experimental import pallas as pl
from jax.experimental.pallas import tpu as pltpu
from jax.sharding import PartitionSpec as P

HD = 128
EPS = 1e-6
NEG = -1e30


def sigma_map(x):
    return jnp.where(x > 0, x + 1.0, jnp.exp(jnp.minimum(x, 0.0)))


def split(x):
    high = x.astype(jnp.bfloat16)
    low = (x - high.astype(jnp.float32)).astype(jnp.bfloat16)
    return high, low


def dot(a, b, dims):
    return lax.dot_general(a, b, (dims, ((), ())), preferred_element_type=jnp.float32)


def carried_head(lines):
    head = lax.axis_index("blk") & 1
    for axis, bit in lines:
        head = head ^ ((lax.axis_index(axis) >> bit) & 1)
    return head


def add_partial(head, k_ref, v_ref):
    cols = pl.ds(pl.multiple_of(head * HD, HD), HD)
    s_hi, s_lo = split(sigma_map(k_ref[:, cols]))
    v_hi, v_lo = split(v_ref[:, cols])
    left = jnp.concatenate([s_hi, s_lo, s_hi], 0)
    right = jnp.concatenate([v_hi, v_hi, v_lo], 0)
    return dot(left, right, ((0,), (0,)))


def chip_kernel(lines, kc_ref, vc_ref, kv_ref, part_ref, kv_out):
    half = kc_ref.shape[1]
    head = carried_head(lines)
    own = add_partial(head, kv_ref.at[:, :half], kv_ref.at[:, half:])
    part_ref[...] = own + add_partial(head, kc_ref, vc_ref)
    kv_out[...] = kv_ref[...]


def combine_kernel(masks, nexts, carries, loose, *refs):
    count = len(masks)
    part_ref = refs[0]
    got_refs = refs[1 : 1 + count]
    outs = refs[1 + count + carries + loose :]
    seg = lax.axis_index("seg")
    total = refs[1 + count][...] if carries else None
    for (s, _), got_ref in zip(masks, got_refs, strict=True):
        got = got_ref[...]
        if not carries:
            got = jnp.where((seg ^ s) < seg, got, 0.0)
        total = got if total is None else total + got
    outs[0][...] = total
    for s, out_ref in zip(nexts, outs[1 : 1 + len(nexts)], strict=True):
        out_ref[...] = total + jnp.where((seg ^ s) > seg, part_ref[...], 0.0)


def attend(q_hi, q_lo, keys, values, mask):
    k_hi, k_lo = split(jnp.concatenate(keys, 0))
    v_hi, v_lo = split(jnp.concatenate(values, 0))
    left = jnp.concatenate([q_hi, q_lo], 1)
    scores = dot(left, jnp.concatenate([k_hi, k_hi], 1), ((1,), (1,)))
    scores = scores + dot(q_hi, k_lo, ((1,), (1,)))
    scores = mask(scores)
    top = jnp.max(scores, axis=1, keepdims=True)
    w = jnp.exp(scores - top)
    total = jnp.sum(w, axis=1, keepdims=True)
    w_hi, w_lo = split(w)
    both = dot(w_hi, jnp.concatenate([v_hi, v_lo], 1), ((1,), (0,)))
    return top, total, both[:, :HD] + both[:, HD:] + dot(w_lo, v_hi, ((1,), (0,)))


def prepare_kernel(group, *refs):
    q_ref, gate_ref, gain_ref = refs[:3]
    qh_ref, ql_ref, sh_ref, sl_ref, mult_ref, keep_ref = refs[3:]
    scale = 1.0 / jnp.sqrt(jnp.float32(HD))
    gates = 1.0 / (1.0 + jnp.exp(-gate_ref[...]))
    for h in range(q_ref.shape[1] // HD):
        s = slice(h * HD, (h + 1) * HD)
        q = q_ref[:, s]
        qh_ref[:, s], ql_ref[:, s] = split(q * scale)
        sh_ref[:, s], sl_ref[:, s] = split(sigma_map(q))
        gate = jnp.broadcast_to(gates[:, h : h + 1], (1, HD))
        mult_ref[:, s] = gate * gain_ref[:, s]
        keep_ref[:, s] = 1.0 - gate


def attention_kernel(group, chunks, *refs):
    qh_ref, ql_ref = refs[:2]
    half = refs[2].shape[1]
    k_refs = [ref.at[:, :half] for ref in refs[4 : 3 + chunks]]
    v_refs = [ref.at[:, half:] for ref in refs[4 : 3 + chunks]]
    k_refs.insert(1, refs[2])
    v_refs.insert(1, refs[3])
    keep_ref, att_ref, done_ref = refs[3 + chunks :]
    rows = qh_ref.shape[0]
    kv_heads = half // HD
    place = lax.axis_index("blk")
    causal = lax.broadcasted_iota(jnp.int32, (rows, rows), 1) <= lax.broadcasted_iota(
        jnp.int32, (rows, rows), 0
    )
    causal = jnp.concatenate([causal] * group, 0)

    def work(count):
        def mask(scores):
            pieces = [jnp.where(causal, scores[:, :rows], NEG)]
            for m in range(1, count // 2):
                piece = scores[:, m * rows : (m + 1) * rows]
                pieces.append(jnp.where((place ^ m) < place, piece, NEG))
            if count > 1:
                pieces.append(scores[:, max(count // 2, 1) * rows :])
            return jnp.concatenate(pieces, 1) if count > 1 else pieces[0]

        for head in range(kv_heads):
            kv = slice(head * HD, (head + 1) * HD)
            spans = [
                slice((head * group + g) * HD, (head * group + g + 1) * HD) for g in range(group)
            ]
            q_hi = jnp.concatenate([qh_ref[:, s] for s in spans], 0)
            q_lo = jnp.concatenate([ql_ref[:, s] for s in spans], 0)
            keys = [k_refs[m][:, kv] for m in range(count)]
            values = [v_refs[m][:, kv] for m in range(count)]
            _, total, accum = attend(q_hi, q_lo, keys, values, mask)
            accum = accum / total
            for g, s in enumerate(spans):
                att_ref[:, s] = accum[g * rows : (g + 1) * rows] * keep_ref[:, s]

    count = 1
    while count <= chunks:
        low, high = count // 2, count
        pl.when((place >= low) & (place < high))(functools.partial(work, count))
        count *= 2
    done_ref[...] = jnp.zeros_like(done_ref)


def final_kernel(group, lines, att_ref, sh_ref, sl_ref, mult_ref, mine_ref, other_ref, out_ref):
    rows = att_ref.shape[0]
    kv_heads = att_ref.shape[1] // (group * HD)
    own = carried_head(lines)
    for head in range(kv_heads):
        memory = jnp.where(own == head, mine_ref[...], other_ref[...])
        m_hi, m_lo = split(memory)
        right = jnp.concatenate([m_hi, m_hi], 0)
        spans = [
            slice((head * group + g) * HD, (head * group + g + 1) * HD) for g in range(group)
        ]
        f_hi = jnp.concatenate([sh_ref[:, s] for s in spans], 0)
        f_lo = jnp.concatenate([sl_ref[:, s] for s in spans], 0)
        r = dot(jnp.concatenate([f_hi, f_lo], 1), right, ((1,), (0,)))
        r = r + dot(f_hi, m_lo, ((1,), (0,)))
        inv = lax.rsqrt(jnp.mean(r * r, axis=1, keepdims=True) + EPS)
        r = r * inv
        for g, s in enumerate(spans):
            out_ref[:, s] = att_ref[:, s] + r[g * rows : (g + 1) * rows] * mult_ref[:, s]


def solution(mesh):
    n_seg, n_blk = mesh.shape["seg"], mesh.shape["blk"]
    both = ("seg", "blk")

    def swap(x, seg_bits, blk_bits):
        pairs = [
            (s * n_blk + b, (s ^ seg_bits) * n_blk + (b ^ blk_bits))
            for s in range(n_seg)
            for b in range(n_blk)
        ]
        return lax.ppermute(x, both, pairs)

    bits = [("seg", i) for i in reversed(range(n_seg.bit_length() - 1))]
    bits += [("blk", i) for i in reversed(range(1, n_blk.bit_length() - 1))]
    groups = [bits[i : i + 2] for i in range(0, len(bits), 2)]
    lines = groups[-1]

    def masks_of(number):
        found = [(0, 0)]
        for axis, bit in reversed(groups[number]):
            flip = int(number == len(groups) - 1)
            step = (1 << bit, flip) if axis == "seg" else (0, (1 << bit) ^ flip)
            found += [(s ^ step[0], b ^ step[1]) for s, b in found]
        return [found[i] for i in ((2, 3, 1) if number == 0 and len(found) > 3 else (3, 2, 1) if len(found) == 4 else range(1, len(found)))]

    def on_device(queries, keys, values, gate_logit, memory_gain):
        rows, width = queries.shape
        group = width // keys.shape[1]
        square = jax.ShapeDtypeStruct((HD, HD), jnp.float32)

        def pass_on(kernel, inputs, loose, passed, outs, flops, passing=pl.BlockSpec(memory_space=pl.ANY)):
            anywhere = pl.BlockSpec(memory_space=pl.ANY)
            count, n_out = len(inputs) + len(loose), len(outs)
            return pl.pallas_call(
                kernel,
                in_specs=[pl.BlockSpec()] * len(inputs) + [anywhere] * len(loose) + [passing] * len(passed),
                out_specs=[pl.BlockSpec()] * n_out + [passing] * len(passed),
                out_shape=outs
                + [jax.ShapeDtypeStruct(x.shape, x.dtype) for x in passed],
                input_output_aliases={count + i: n_out + i for i in range(len(passed))},
                compiler_params=pltpu.CompilerParams(vmem_limit_bytes=8 * 1024 * 1024),
                cost_estimate=pl.CostEstimate(
                    flops=flops, bytes_accessed=500_000, transcendentals=20_000
                ),
            )(*inputs, *loose, *passed)

        k_core, v_core = swap(keys, 0, 1), swap(values, 0, 1)
        own = jnp.concatenate([keys, values], 1)
        part, own = pass_on(
            functools.partial(chip_kernel, lines), [k_core, v_core], [], [own], [square], 500_000_000, pl.BlockSpec()
        )
        gate, gain = gate_logit.reshape(1, -1), memory_gain.reshape(1, -1)
        wide = jax.ShapeDtypeStruct((rows, width), jnp.float32)
        half = jax.ShapeDtypeStruct((rows, width), jnp.bfloat16)
        line = jax.ShapeDtypeStruct((1, width), jnp.float32)
        large = pltpu.CompilerParams(vmem_limit_bytes=24 * 1024 * 1024)
        q_hi, q_lo, f_hi, f_lo, mult, keep = pl.pallas_call(
            functools.partial(prepare_kernel, group),
            out_shape=(half, half, half, half, line, line),
            compiler_params=large,
            cost_estimate=pl.CostEstimate(
                flops=1_000_000, bytes_accessed=100_000, transcendentals=0
            ),
        )(queries, gate, gain)

        held = [own, None]
        fresh = [swap(own, 0, 2)] if n_blk > 2 else []

        carried = None
        sends = {s: part for s, _ in masks_of(0)}
        for number in range(len(groups)):
            masks = masks_of(number)
            got = [swap(sends[s], s, b) for s, b in masks]
            last = number == len(groups) - 1
            nexts = [] if last else sorted({s for s, _ in masks_of(number + 1) if s})
            some = [] if carried is None else [carried]
            loose = [mult] if number == 0 else [done] if last else []
            carried, *extra = pass_on(
                functools.partial(combine_kernel, masks, nexts, len(some), len(loose)),
                [part, *got, *some],
                loose,
                [],
                [square] * (1 + len(nexts)),
                10_000_000_000 if number == 0 else 100_000,
            )
            sends = {0: carried, **dict(zip(nexts, extra, strict=True))}
            if number == 0:
                step = 2
                while step < n_blk:
                    news = fresh if step == 2 else [swap(held[m], 0, step) for m in range(0, step, 2)]
                    for new in news:
                        held += [new, swap(new, 0, 1)]
                    step *= 2
                att, done = pl.pallas_call(
                    functools.partial(attention_kernel, group, n_blk),
                    out_shape=(wide, jax.ShapeDtypeStruct((8, HD), jnp.float32)),
                    compiler_params=large,
                    cost_estimate=pl.CostEstimate(
                        flops=1_000_000, bytes_accessed=100_000, transcendentals=0
                    ),
                )(q_hi, q_lo, k_core, v_core, own, *held[2:], keep)
        other = swap(carried, 0, 1)

        return pl.pallas_call(
            functools.partial(final_kernel, group, lines),
            out_shape=jax.ShapeDtypeStruct((rows, width), jnp.float32),
            compiler_params=pltpu.CompilerParams(vmem_limit_bytes=16 * 1024 * 1024),
        )(att, f_hi, f_lo, mult, carried, other)

    return jax.shard_map(
        on_device,
        mesh=mesh,
        in_specs=(P(both, None), P(both, None), P(both, None), P(), P()),
        out_specs=P(both, None),
        check_vma=False,
    )
```

```python
import functools

import jax
import jax.numpy as jnp
from jax import lax
from jax.experimental import pallas as pl
from jax.experimental.pallas import tpu as pltpu
from jax.sharding import PartitionSpec as P

HD = 128
EPS = 1e-6
NEG = -1e30


def sigma_map(x):
    return jnp.where(x > 0, x + 1.0, jnp.exp(jnp.minimum(x, 0.0)))


def split(x):
    high = x.astype(jnp.bfloat16)
    low = (x - high.astype(jnp.float32)).astype(jnp.bfloat16)
    return high, low


def dot(a, b, dims):
    return lax.dot_general(a, b, (dims, ((), ())), preferred_element_type=jnp.float32)


def carried_head(lines):
    head = lax.axis_index("blk") & 1
    for axis, bit in lines:
        head = head ^ ((lax.axis_index(axis) >> bit) & 1)
    return head


def add_partial(head, k_ref, v_ref):
    cols = pl.ds(pl.multiple_of(head * HD, HD), HD)
    s_hi, s_lo = split(sigma_map(k_ref[:, cols]))
    v_hi, v_lo = split(v_ref[:, cols])
    left = jnp.concatenate([s_hi, s_lo, s_hi], 0)
    right = jnp.concatenate([v_hi, v_hi, v_lo], 0)
    return dot(left, right, ((0,), (0,)))


def chip_kernel(lines, kc_ref, vc_ref, kv_ref, part_ref, kv_out):
    half = kc_ref.shape[1]
    head = carried_head(lines)
    own = add_partial(head, kv_ref.at[:, :half], kv_ref.at[:, half:])
    part_ref[...] = own + add_partial(head, kc_ref, vc_ref)
    kv_out[...] = kv_ref[...]


def combine_kernel(masks, nexts, carries, loose, *refs):
    count = len(masks)
    part_ref = refs[0]
    got_refs = refs[1 : 1 + count]
    outs = refs[1 + count + carries + loose :]
    seg = lax.axis_index("seg")
    total = refs[1 + count][...] if carries else None
    for (s, _), got_ref in zip(masks, got_refs, strict=True):
        got = got_ref[...]
        if not carries:
            got = jnp.where((seg ^ s) < seg, got, 0.0)
        total = got if total is None else total + got
    outs[0][...] = total
    for s, out_ref in zip(nexts, outs[1 : 1 + len(nexts)], strict=True):
        out_ref[...] = total + jnp.where((seg ^ s) > seg, part_ref[...], 0.0)


def attend(q_hi, q_lo, keys, values, mask):
    k_hi, k_lo = split(jnp.concatenate(keys, 0))
    v_hi, v_lo = split(jnp.concatenate(values, 0))
    left = jnp.concatenate([q_hi, q_lo], 1)
    scores = dot(left, jnp.concatenate([k_hi, k_hi], 1), ((1,), (1,)))
    scores = scores + dot(q_hi, k_lo, ((1,), (1,)))
    scores = mask(scores)
    top = jnp.max(scores, axis=1, keepdims=True)
    w = jnp.exp(scores - top)
    total = jnp.sum(w, axis=1, keepdims=True)
    w_hi, w_lo = split(w)
    both = dot(w_hi, jnp.concatenate([v_hi, v_lo], 1), ((1,), (0,)))
    return top, total, both[:, :HD] + both[:, HD:] + dot(w_lo, v_hi, ((1,), (0,)))


def prepare_kernel(group, *refs):
    q_ref, gate_ref, gain_ref = refs[:3]
    qh_ref, ql_ref, sh_ref, sl_ref, mult_ref, keep_ref = refs[3:]
    scale = 1.0 / jnp.sqrt(jnp.float32(HD))
    gates = 1.0 / (1.0 + jnp.exp(-gate_ref[...]))
    for h in range(q_ref.shape[1] // HD):
        s = slice(h * HD, (h + 1) * HD)
        q = q_ref[:, s]
        qh_ref[:, s], ql_ref[:, s] = split(q * scale)
        sh_ref[:, s], sl_ref[:, s] = split(sigma_map(q))
        gate = jnp.broadcast_to(gates[:, h : h + 1], (1, HD))
        mult_ref[:, s] = gate * gain_ref[:, s]
        keep_ref[:, s] = 1.0 - gate


def attention_kernel(group, chunks, *refs):
    qh_ref, ql_ref = refs[:2]
    half = refs[2].shape[1]
    k_refs = [ref.at[:, :half] for ref in refs[4 : 3 + chunks]]
    v_refs = [ref.at[:, half:] for ref in refs[4 : 3 + chunks]]
    k_refs.insert(1, refs[2])
    v_refs.insert(1, refs[3])
    keep_ref, att_ref, done_ref = refs[3 + chunks :]
    rows = qh_ref.shape[0]
    kv_heads = half // HD
    place = lax.axis_index("blk")
    causal = lax.broadcasted_iota(jnp.int32, (rows, rows), 1) <= lax.broadcasted_iota(
        jnp.int32, (rows, rows), 0
    )
    causal = jnp.concatenate([causal] * group, 0)

    def work(count):
        def mask(scores):
            pieces = [jnp.where(causal, scores[:, :rows], NEG)]
            for m in range(1, count // 2):
                piece = scores[:, m * rows : (m + 1) * rows]
                pieces.append(jnp.where((place ^ m) < place, piece, NEG))
            if count > 1:
                pieces.append(scores[:, max(count // 2, 1) * rows :])
            return jnp.concatenate(pieces, 1) if count > 1 else pieces[0]

        for head in range(kv_heads):
            kv = slice(head * HD, (head + 1) * HD)
            spans = [
                slice((head * group + g) * HD, (head * group + g + 1) * HD) for g in range(group)
            ]
            q_hi = jnp.concatenate([qh_ref[:, s] for s in spans], 0)
            q_lo = jnp.concatenate([ql_ref[:, s] for s in spans], 0)
            keys = [k_refs[m][:, kv] for m in range(count)]
            values = [v_refs[m][:, kv] for m in range(count)]
            _, total, accum = attend(q_hi, q_lo, keys, values, mask)
            accum = accum / total
            for g, s in enumerate(spans):
                att_ref[:, s] = accum[g * rows : (g + 1) * rows] * keep_ref[:, s]

    count = 1
    while count <= chunks:
        low, high = count // 2, count
        pl.when((place >= low) & (place < high))(functools.partial(work, count))
        count *= 2
    done_ref[...] = jnp.zeros_like(done_ref)


def mix_head(group, first, att_ref, sh_ref, sl_ref, mult_ref, memory_ref):
    rows = att_ref.shape[0]
    m_hi, m_lo = split(memory_ref[...])
    spans = [pl.ds(pl.multiple_of((first + g) * HD, HD), HD) for g in range(group)]
    f_hi = jnp.concatenate([sh_ref[:, s] for s in spans], 0)
    f_lo = jnp.concatenate([sl_ref[:, s] for s in spans], 0)
    r = dot(jnp.concatenate([f_hi, f_lo], 1), jnp.concatenate([m_hi, m_hi], 0), ((1,), (0,)))
    r = r + dot(f_hi, m_lo, ((1,), (0,)))
    r = r * lax.rsqrt(jnp.mean(r * r, axis=1, keepdims=True) + EPS)
    return [
        (s, att_ref[:, s] + r[g * rows : (g + 1) * rows] * mult_ref[:, s])
        for g, s in enumerate(spans)
    ]


def own_mix_kernel(group, lines, *refs):
    for g, (_, mixed) in enumerate(mix_head(group, carried_head(lines) * group, *refs[:5])):
        refs[5][g] = mixed


def final_kernel(group, lines, *refs):
    ready_ref, out_ref, tile_ref, sems = refs[5:]
    own = carried_head(lines)
    copies = []
    for g in range(group):
        s = pl.ds(pl.multiple_of((own * group + g) * HD, HD), HD)
        copies.append(pltpu.make_async_copy(ready_ref.at[g], out_ref.at[:, s], sems.at[g]))
        copies[-1].start()
    for g, (s, mixed) in enumerate(mix_head(group, (1 - own) * group, *refs[:5])):
        tile_ref[g] = mixed
        copies.append(pltpu.make_async_copy(tile_ref.at[g], out_ref.at[:, s], sems.at[group + g]))
        copies[-1].start()
    for copy in copies:
        copy.wait()


def solution(mesh):
    n_seg, n_blk = mesh.shape["seg"], mesh.shape["blk"]
    both = ("seg", "blk")

    def swap(x, seg_bits, blk_bits):
        pairs = [
            (s * n_blk + b, (s ^ seg_bits) * n_blk + (b ^ blk_bits))
            for s in range(n_seg)
            for b in range(n_blk)
        ]
        return lax.ppermute(x, both, pairs)

    bits = [("seg", i) for i in reversed(range(n_seg.bit_length() - 1))]
    bits += [("blk", i) for i in reversed(range(1, n_blk.bit_length() - 1))]
    groups = [bits[i : i + 2] for i in range(0, len(bits), 2)]
    lines = groups[-1]

    def masks_of(number):
        found = [(0, 0)]
        for axis, bit in reversed(groups[number]):
            flip = int(number == len(groups) - 1)
            step = (1 << bit, flip) if axis == "seg" else (0, (1 << bit) ^ flip)
            found += [(s ^ step[0], b ^ step[1]) for s, b in found]
        return [found[i] for i in ((2, 3, 1) if number == 0 and len(found) > 3 else (3, 2, 1) if len(found) == 4 else range(1, len(found)))]

    def on_device(queries, keys, values, gate_logit, memory_gain):
        rows, width = queries.shape
        group = width // keys.shape[1]
        square = jax.ShapeDtypeStruct((HD, HD), jnp.float32)

        def pass_on(kernel, inputs, loose, passed, outs, flops, passing=pl.BlockSpec(memory_space=pl.ANY)):
            anywhere = pl.BlockSpec(memory_space=pl.ANY)
            count, n_out = len(inputs) + len(loose), len(outs)
            return pl.pallas_call(
                kernel,
                in_specs=[pl.BlockSpec()] * len(inputs) + [anywhere] * len(loose) + [passing] * len(passed),
                out_specs=[pl.BlockSpec()] * n_out + [passing] * len(passed),
                out_shape=outs
                + [jax.ShapeDtypeStruct(x.shape, x.dtype) for x in passed],
                input_output_aliases={count + i: n_out + i for i in range(len(passed))},
                compiler_params=pltpu.CompilerParams(vmem_limit_bytes=8 * 1024 * 1024),
                cost_estimate=pl.CostEstimate(
                    flops=flops, bytes_accessed=500_000, transcendentals=20_000
                ),
            )(*inputs, *loose, *passed)

        k_core, v_core = swap(keys, 0, 1), swap(values, 0, 1)
        own = jnp.concatenate([keys, values], 1)
        part, own = pass_on(
            functools.partial(chip_kernel, lines), [k_core, v_core], [], [own], [square], 500_000_000, pl.BlockSpec()
        )
        gate, gain = gate_logit.reshape(1, -1), memory_gain.reshape(1, -1)
        wide = jax.ShapeDtypeStruct((rows, width), jnp.float32)
        half = jax.ShapeDtypeStruct((rows, width), jnp.bfloat16)
        line = jax.ShapeDtypeStruct((1, width), jnp.float32)
        large = pltpu.CompilerParams(vmem_limit_bytes=24 * 1024 * 1024)
        q_hi, q_lo, f_hi, f_lo, mult, keep = pl.pallas_call(
            functools.partial(prepare_kernel, group),
            out_shape=(half, half, half, half, line, line),
            compiler_params=large,
            cost_estimate=pl.CostEstimate(
                flops=1_000_000, bytes_accessed=100_000, transcendentals=0
            ),
        )(queries, gate, gain)

        held = [own, None]
        fresh = [swap(own, 0, 2)] if n_blk > 2 else []

        carried = None
        sends = {s: part for s, _ in masks_of(0)}
        for number in range(len(groups)):
            masks = masks_of(number)
            got = [swap(sends[s], s, b) for s, b in masks]
            last = number == len(groups) - 1
            nexts = [] if last else sorted({s for s, _ in masks_of(number + 1) if s})
            some = [] if carried is None else [carried]
            loose = [mult] if number == 0 else [done] if last else []
            carried, *extra = pass_on(
                functools.partial(combine_kernel, masks, nexts, len(some), len(loose)),
                [part, *got, *some],
                loose,
                [],
                [square] * (1 + len(nexts)),
                10_000_000_000 if number == 0 else 100_000,
            )
            sends = {0: carried, **dict(zip(nexts, extra, strict=True))}
            if number == 0:
                step = 2
                while step < n_blk:
                    news = fresh if step == 2 else [swap(held[m], 0, step) for m in range(0, step, 2)]
                    for new in news:
                        held += [new, swap(new, 0, 1)]
                    step *= 2
                att, done = pl.pallas_call(
                    functools.partial(attention_kernel, group, n_blk),
                    out_shape=(wide, jax.ShapeDtypeStruct((8, HD), jnp.float32)),
                    compiler_params=large,
                    cost_estimate=pl.CostEstimate(
                        flops=1_000_000, bytes_accessed=100_000, transcendentals=0
                    ),
                )(q_hi, q_lo, k_core, v_core, own, *held[2:], keep)
        other = swap(carried, 0, 1)

        tiles = (group, rows, HD)
        small = pltpu.CompilerParams(vmem_limit_bytes=16 * 1024 * 1024)
        ready = pl.pallas_call(
            functools.partial(own_mix_kernel, group, lines),
            out_shape=jax.ShapeDtypeStruct(tiles, jnp.float32),
            compiler_params=small,
            cost_estimate=pl.CostEstimate(
                flops=1_000_000_000, bytes_accessed=500_000, transcendentals=0
            ),
        )(att, f_hi, f_lo, mult, carried)
        return pl.pallas_call(
            functools.partial(final_kernel, group, lines),
            out_specs=pl.BlockSpec(memory_space=pl.ANY),
            out_shape=wide,
            scratch_shapes=[
                pltpu.VMEM(tiles, jnp.float32),
                pltpu.SemaphoreType.DMA((2 * group,)),
            ],
            compiler_params=small,
        )(att, f_hi, f_lo, mult, other, ready)

    return jax.shard_map(
        on_device,
        mesh=mesh,
        in_specs=(P(both, None), P(both, None), P(both, None), P(), P()),
        out_specs=P(both, None),
        check_vma=False,
    )
```

```python
import functools

import jax
import jax.numpy as jnp
from jax import lax
from jax.experimental import pallas as pl
from jax.experimental.pallas import tpu as pltpu
from jax.sharding import PartitionSpec as P

HD = 128
EPS = 1e-6
NEG = -1e30


def sigma_map(x):
    return jnp.where(x > 0, x + 1.0, jnp.exp(jnp.minimum(x, 0.0)))


def split(x):
    high = x.astype(jnp.bfloat16)
    low = (x - high.astype(jnp.float32)).astype(jnp.bfloat16)
    return high, low


def dot(a, b, dims):
    return lax.dot_general(a, b, (dims, ((), ())), preferred_element_type=jnp.float32)


def carried_head(lines):
    head = lax.axis_index("blk") & 1
    for axis, bit in lines:
        head = head ^ ((lax.axis_index(axis) >> bit) & 1)
    return head


def add_partial(head, k_ref, v_ref):
    cols = pl.ds(pl.multiple_of(head * HD, HD), HD)
    s_hi, s_lo = split(sigma_map(k_ref[:, cols]))
    v_hi, v_lo = split(v_ref[:, cols])
    left = jnp.concatenate([s_hi, s_lo, s_hi], 0)
    right = jnp.concatenate([v_hi, v_hi, v_lo], 0)
    return dot(left, right, ((0,), (0,)))


def chip_kernel(lines, kc_ref, vc_ref, kv_ref, part_ref, kv_out):
    half = kc_ref.shape[1]
    head = carried_head(lines)
    own = add_partial(head, kv_ref.at[:, :half], kv_ref.at[:, half:])
    part_ref[...] = own + add_partial(head, kc_ref, vc_ref)
    kv_out[...] = kv_ref[...]


def combine_kernel(masks, nexts, carries, loose, *refs):
    count = len(masks)
    part_ref = refs[0]
    got_refs = refs[1 : 1 + count]
    outs = refs[1 + count + carries + loose :]
    seg = lax.axis_index("seg")
    total = refs[1 + count][...] if carries else None
    for (s, _), got_ref in zip(masks, got_refs, strict=True):
        got = got_ref[...]
        if not carries:
            got = jnp.where((seg ^ s) < seg, got, 0.0)
        total = got if total is None else total + got
    outs[0][...] = total
    for s, out_ref in zip(nexts, outs[1 : 1 + len(nexts)], strict=True):
        out_ref[...] = total + jnp.where((seg ^ s) > seg, part_ref[...], 0.0)


def attend(q_hi, q_lo, keys, values, mask):
    k_hi, k_lo = split(jnp.concatenate(keys, 0))
    v_hi, v_lo = split(jnp.concatenate(values, 0))
    left = jnp.concatenate([q_hi, q_lo], 1)
    scores = dot(left, jnp.concatenate([k_hi, k_hi], 1), ((1,), (1,)))
    scores = scores + dot(q_hi, k_lo, ((1,), (1,)))
    scores = mask(scores)
    top = jnp.max(scores, axis=1, keepdims=True)
    w = jnp.exp(scores - top)
    total = jnp.sum(w, axis=1, keepdims=True)
    w_hi, w_lo = split(w)
    both = dot(w_hi, jnp.concatenate([v_hi, v_lo], 1), ((1,), (0,)))
    return top, total, both[:, :HD] + both[:, HD:] + dot(w_lo, v_hi, ((1,), (0,)))


def prepare_kernel(group, *refs):
    q_ref, gate_ref, gain_ref = refs[:3]
    qh_ref, ql_ref, sh_ref, sl_ref, mult_ref, keep_ref = refs[3:]
    scale = 1.0 / jnp.sqrt(jnp.float32(HD))
    gates = 1.0 / (1.0 + jnp.exp(-gate_ref[...]))
    for h in range(q_ref.shape[1] // HD):
        s = slice(h * HD, (h + 1) * HD)
        q = q_ref[:, s]
        qh_ref[:, s], ql_ref[:, s] = split(q * scale)
        sh_ref[:, s], sl_ref[:, s] = split(sigma_map(q))
        gate = jnp.broadcast_to(gates[:, h : h + 1], (1, HD))
        mult_ref[:, s] = gate * gain_ref[:, s]
        keep_ref[:, s] = 1.0 - gate


def attention_kernel(group, chunks, *refs):
    qh_ref, ql_ref = refs[:2]
    half = refs[2].shape[1]
    k_refs = [ref.at[:, :half] for ref in refs[4 : 3 + chunks]]
    v_refs = [ref.at[:, half:] for ref in refs[4 : 3 + chunks]]
    k_refs.insert(1, refs[2])
    v_refs.insert(1, refs[3])
    keep_ref, att_ref, done_ref = refs[3 + chunks :]
    rows = qh_ref.shape[0]
    kv_heads = half // HD
    place = lax.axis_index("blk")
    causal = lax.broadcasted_iota(jnp.int32, (rows, rows), 1) <= lax.broadcasted_iota(
        jnp.int32, (rows, rows), 0
    )
    causal = jnp.concatenate([causal] * group, 0)

    def work(count):
        def mask(scores):
            pieces = [jnp.where(causal, scores[:, :rows], NEG)]
            for m in range(1, count // 2):
                piece = scores[:, m * rows : (m + 1) * rows]
                pieces.append(jnp.where((place ^ m) < place, piece, NEG))
            if count > 1:
                pieces.append(scores[:, max(count // 2, 1) * rows :])
            return jnp.concatenate(pieces, 1) if count > 1 else pieces[0]

        for head in range(kv_heads):
            kv = slice(head * HD, (head + 1) * HD)
            spans = [
                slice((head * group + g) * HD, (head * group + g + 1) * HD) for g in range(group)
            ]
            q_hi = jnp.concatenate([qh_ref[:, s] for s in spans], 0)
            q_lo = jnp.concatenate([ql_ref[:, s] for s in spans], 0)
            keys = [k_refs[m][:, kv] for m in range(count)]
            values = [v_refs[m][:, kv] for m in range(count)]
            _, total, accum = attend(q_hi, q_lo, keys, values, mask)
            accum = accum / total
            for g, s in enumerate(spans):
                att_ref[:, s] = accum[g * rows : (g + 1) * rows] * keep_ref[:, s]

    count = 1
    while count <= chunks:
        low, high = count // 2, count
        pl.when((place >= low) & (place < high))(functools.partial(work, count))
        count *= 2
    done_ref[...] = jnp.zeros_like(done_ref)


def mix_head(group, first, att_ref, sh_ref, sl_ref, mult_ref, memory_ref):
    rows = att_ref.shape[0]
    m_hi, m_lo = split(memory_ref[...])
    spans = [pl.ds(pl.multiple_of((first + g) * HD, HD), HD) for g in range(group)]
    f_hi = jnp.concatenate([sh_ref[:, s] for s in spans], 0)
    f_lo = jnp.concatenate([sl_ref[:, s] for s in spans], 0)
    r = dot(jnp.concatenate([f_hi, f_lo], 1), jnp.concatenate([m_hi, m_hi], 0), ((1,), (0,)))
    r = r + dot(f_hi, m_lo, ((1,), (0,)))
    r = r * lax.rsqrt(jnp.mean(r * r, axis=1, keepdims=True) + EPS)
    return [
        (s, att_ref[:, s] + r[g * rows : (g + 1) * rows] * mult_ref[:, s])
        for g, s in enumerate(spans)
    ]


def own_mix_kernel(group, lines, *refs):
    for g, (_, mixed) in enumerate(mix_head(group, carried_head(lines) * group, *refs[:5])):
        refs[5][g] = mixed


def final_kernel(group, lines, *refs):
    ready_ref, out_ref, tile_ref, sems = refs[5:]
    own = carried_head(lines)
    copies = []
    for g in range(group):
        s = pl.ds(pl.multiple_of((own * group + g) * HD, HD), HD)
        copies.append(pltpu.make_async_copy(ready_ref.at[g], out_ref.at[:, s], sems.at[g]))
        copies[-1].start()
    for g, (s, mixed) in enumerate(mix_head(group, (1 - own) * group, *refs[:5])):
        tile_ref[g] = mixed
        copies.append(pltpu.make_async_copy(tile_ref.at[g], out_ref.at[:, s], sems.at[group + g]))
        copies[-1].start()
    for copy in copies:
        copy.wait()


def solution(mesh):
    n_seg, n_blk = mesh.shape["seg"], mesh.shape["blk"]
    both = ("seg", "blk")

    def swap(x, seg_bits, blk_bits):
        pairs = [
            (s * n_blk + b, (s ^ seg_bits) * n_blk + (b ^ blk_bits))
            for s in range(n_seg)
            for b in range(n_blk)
        ]
        return lax.ppermute(x, both, pairs)

    bits = [("seg", i) for i in reversed(range(n_seg.bit_length() - 1))]
    bits += [("blk", i) for i in reversed(range(1, n_blk.bit_length() - 1))]
    groups = [bits[i : i + 2] for i in range(0, len(bits), 2)]
    flips = dict(zip(groups[0], (0, 0), strict=False))
    flips.update(zip(groups[-1], (0, 1), strict=False))
    lines = [line for line in bits if flips.get(line)]

    def masks_of(number):
        found = [(0, 0)]
        for axis, bit in reversed(groups[number]):
            flip = flips.get((axis, bit), 0)
            step = (1 << bit, flip) if axis == "seg" else (0, (1 << bit) ^ flip)
            found += [(s ^ step[0], b ^ step[1]) for s, b in found]
        return [found[i] for i in ((2, 3, 1) if number == 0 and len(found) > 3 else (3, 2, 1) if len(found) == 4 else range(1, len(found)))]

    def on_device(queries, keys, values, gate_logit, memory_gain):
        rows, width = queries.shape
        group = width // keys.shape[1]
        square = jax.ShapeDtypeStruct((HD, HD), jnp.float32)

        def pass_on(kernel, inputs, loose, passed, outs, flops, passing=pl.BlockSpec(memory_space=pl.ANY)):
            anywhere = pl.BlockSpec(memory_space=pl.ANY)
            count, n_out = len(inputs) + len(loose), len(outs)
            return pl.pallas_call(
                kernel,
                in_specs=[pl.BlockSpec()] * len(inputs) + [anywhere] * len(loose) + [passing] * len(passed),
                out_specs=[pl.BlockSpec()] * n_out + [passing] * len(passed),
                out_shape=outs
                + [jax.ShapeDtypeStruct(x.shape, x.dtype) for x in passed],
                input_output_aliases={count + i: n_out + i for i in range(len(passed))},
                compiler_params=pltpu.CompilerParams(vmem_limit_bytes=8 * 1024 * 1024),
                cost_estimate=pl.CostEstimate(
                    flops=flops, bytes_accessed=500_000, transcendentals=20_000
                ),
            )(*inputs, *loose, *passed)

        k_core, v_core = swap(keys, 0, 1), swap(values, 0, 1)
        own = jnp.concatenate([keys, values], 1)
        part, own = pass_on(
            functools.partial(chip_kernel, lines), [k_core, v_core], [], [own], [square], 500_000_000, pl.BlockSpec()
        )
        gate, gain = gate_logit.reshape(1, -1), memory_gain.reshape(1, -1)
        wide = jax.ShapeDtypeStruct((rows, width), jnp.float32)
        half = jax.ShapeDtypeStruct((rows, width), jnp.bfloat16)
        line = jax.ShapeDtypeStruct((1, width), jnp.float32)
        large = pltpu.CompilerParams(vmem_limit_bytes=24 * 1024 * 1024)
        q_hi, q_lo, f_hi, f_lo, mult, keep = pl.pallas_call(
            functools.partial(prepare_kernel, group),
            out_shape=(half, half, half, half, line, line),
            compiler_params=large,
            cost_estimate=pl.CostEstimate(
                flops=1_000_000, bytes_accessed=100_000, transcendentals=0
            ),
        )(queries, gate, gain)

        held = [own, None]
        fresh = [swap(own, 0, 3)] if n_blk > 2 else []

        carried = None
        sends = {s: part for s, _ in masks_of(0)}
        for number in range(len(groups)):
            masks = masks_of(number)
            got = [swap(sends[s], s, b) for s, b in masks]
            last = number == len(groups) - 1
            nexts = [] if last else sorted({s for s, _ in masks_of(number + 1) if s})
            some = [] if carried is None else [carried]
            loose = [mult] if number == 0 else [done] if last else []
            carried, *extra = pass_on(
                functools.partial(combine_kernel, masks, nexts, len(some), len(loose)),
                [part, *got, *some],
                loose,
                [],
                [square] * (1 + len(nexts)),
                10_000_000_000 if number == 0 else 100_000,
            )
            sends = {0: carried, **dict(zip(nexts, extra, strict=True))}
            if number == 0:
                step = 2
                while step < n_blk:
                    news = fresh if step == 2 else [swap(held[m], 0, step) for m in range(0, step, 2)]
                    for new in news:
                        near = swap(new, 0, 1)
                        held += [near, new] if step == 2 else [new, near]
                    step *= 2
                att, done = pl.pallas_call(
                    functools.partial(attention_kernel, group, n_blk),
                    out_shape=(wide, jax.ShapeDtypeStruct((8, HD), jnp.float32)),
                    compiler_params=large,
                    cost_estimate=pl.CostEstimate(
                        flops=1_000_000, bytes_accessed=100_000, transcendentals=0
                    ),
                )(q_hi, q_lo, k_core, v_core, own, *held[2:], keep)
        other = swap(carried, 0, 1)

        tiles = (group, rows, HD)
        small = pltpu.CompilerParams(vmem_limit_bytes=16 * 1024 * 1024)
        ready = pl.pallas_call(
            functools.partial(own_mix_kernel, group, lines),
            out_shape=jax.ShapeDtypeStruct(tiles, jnp.float32),
            compiler_params=small,
            cost_estimate=pl.CostEstimate(
                flops=1_000_000_000, bytes_accessed=500_000, transcendentals=0
            ),
        )(att, f_hi, f_lo, mult, carried)
        return pl.pallas_call(
            functools.partial(final_kernel, group, lines),
            out_specs=pl.BlockSpec(memory_space=pl.ANY),
            out_shape=wide,
            scratch_shapes=[
                pltpu.VMEM(tiles, jnp.float32),
                pltpu.SemaphoreType.DMA((2 * group,)),
            ],
            compiler_params=small,
        )(att, f_hi, f_lo, mult, other, ready)

    return jax.shard_map(
        on_device,
        mesh=mesh,
        in_specs=(P(both, None), P(both, None), P(both, None), P(), P()),
        out_specs=P(both, None),
        check_vma=False,
    )
```

```python
import functools

import jax
import jax.numpy as jnp
from jax import lax
from jax.experimental import pallas as pl
from jax.experimental.pallas import tpu as pltpu
from jax.sharding import PartitionSpec as P

HD = 128
EPS = 1e-6
NEG = -1e30


def sigma_map(x):
    return jnp.where(x > 0, x + 1.0, jnp.exp(jnp.minimum(x, 0.0)))


def split(x):
    high = x.astype(jnp.bfloat16)
    low = (x - high.astype(jnp.float32)).astype(jnp.bfloat16)
    return high, low


def dot(a, b, dims):
    return lax.dot_general(a, b, (dims, ((), ())), preferred_element_type=jnp.float32)


def carried_head(lines):
    head = lax.axis_index("blk") & 1
    for axis, bit in lines:
        head = head ^ ((lax.axis_index(axis) >> bit) & 1)
    return head


def add_partial(head, k_ref, v_ref):
    cols = pl.ds(pl.multiple_of(head * HD, HD), HD)
    s_hi, s_lo = split(sigma_map(k_ref[:, cols]))
    v_hi, v_lo = split(v_ref[:, cols])
    left = jnp.concatenate([s_hi, s_lo, s_hi], 0)
    right = jnp.concatenate([v_hi, v_hi, v_lo], 0)
    return dot(left, right, ((0,), (0,)))


def chip_kernel(lines, kc_ref, vc_ref, kv_ref, part_ref, kv_out):
    half = kc_ref.shape[1]
    head = carried_head(lines)
    own = add_partial(head, kv_ref.at[:, :half], kv_ref.at[:, half:])
    part_ref[...] = own + add_partial(head, kc_ref, vc_ref)
    kv_out[...] = kv_ref[...]


def combine_kernel(masks, nexts, carries, loose, *refs):
    count = len(masks)
    part_ref = refs[0]
    got_refs = refs[1 : 1 + count]
    outs = refs[1 + count + carries + loose :]
    seg = lax.axis_index("seg")
    total = refs[1 + count][...] if carries else None
    for (s, _), got_ref in zip(masks, got_refs, strict=True):
        got = got_ref[...]
        if not carries:
            got = jnp.where((seg ^ s) < seg, got, 0.0)
        total = got if total is None else total + got
    outs[0][...] = total
    for s, out_ref in zip(nexts, outs[1 : 1 + len(nexts)], strict=True):
        out_ref[...] = total + jnp.where((seg ^ s) > seg, part_ref[...], 0.0)


def attend(q_hi, q_lo, keys, values, mask):
    k_hi, k_lo = split(jnp.concatenate(keys, 0))
    v_hi, v_lo = split(jnp.concatenate(values, 0))
    left = jnp.concatenate([q_hi, q_lo], 1)
    scores = dot(left, jnp.concatenate([k_hi, k_hi], 1), ((1,), (1,)))
    scores = scores + dot(q_hi, k_lo, ((1,), (1,)))
    scores = mask(scores)
    top = jnp.max(scores, axis=1, keepdims=True)
    w = jnp.exp(scores - top)
    total = jnp.sum(w, axis=1, keepdims=True)
    w_hi, w_lo = split(w)
    both = dot(w_hi, jnp.concatenate([v_hi, v_lo], 1), ((1,), (0,)))
    return top, total, both[:, :HD] + both[:, HD:] + dot(w_lo, v_hi, ((1,), (0,)))


def prepare_kernel(group, *refs):
    q_ref, gate_ref, gain_ref = refs[:3]
    qh_ref, ql_ref, sh_ref, sl_ref, mult_ref, keep_ref = refs[3:]
    scale = 1.0 / jnp.sqrt(jnp.float32(HD))
    gates = 1.0 / (1.0 + jnp.exp(-gate_ref[...]))
    for h in range(q_ref.shape[1] // HD):
        s = slice(h * HD, (h + 1) * HD)
        q = q_ref[:, s]
        qh_ref[:, s], ql_ref[:, s] = split(q * scale)
        sh_ref[:, s], sl_ref[:, s] = split(sigma_map(q))
        gate = jnp.broadcast_to(gates[:, h : h + 1], (1, HD))
        mult_ref[:, s] = gate * gain_ref[:, s]
        keep_ref[:, s] = 1.0 - gate


def attention_kernel(group, chunks, *refs):
    qh_ref, ql_ref = refs[:2]
    half = refs[2].shape[1]
    k_refs = [ref.at[:, :half] for ref in refs[4 : 3 + chunks]]
    v_refs = [ref.at[:, half:] for ref in refs[4 : 3 + chunks]]
    k_refs.insert(1, refs[2])
    v_refs.insert(1, refs[3])
    keep_ref, att_ref, done_ref = refs[3 + chunks :]
    rows = qh_ref.shape[0]
    kv_heads = half // HD
    place = lax.axis_index("blk")
    causal = lax.broadcasted_iota(jnp.int32, (rows, rows), 1) <= lax.broadcasted_iota(
        jnp.int32, (rows, rows), 0
    )
    causal = jnp.concatenate([causal] * group, 0)

    def work(count):
        def mask(scores):
            pieces = [jnp.where(causal, scores[:, :rows], NEG)]
            for m in range(1, count // 2):
                piece = scores[:, m * rows : (m + 1) * rows]
                pieces.append(jnp.where((place ^ m) < place, piece, NEG))
            if count > 1:
                pieces.append(scores[:, max(count // 2, 1) * rows :])
            return jnp.concatenate(pieces, 1) if count > 1 else pieces[0]

        for head in range(kv_heads):
            kv = slice(head * HD, (head + 1) * HD)
            spans = [
                slice((head * group + g) * HD, (head * group + g + 1) * HD) for g in range(group)
            ]
            q_hi = jnp.concatenate([qh_ref[:, s] for s in spans], 0)
            q_lo = jnp.concatenate([ql_ref[:, s] for s in spans], 0)
            keys = [k_refs[m][:, kv] for m in range(count)]
            values = [v_refs[m][:, kv] for m in range(count)]
            _, total, accum = attend(q_hi, q_lo, keys, values, mask)
            accum = accum / total
            for g, s in enumerate(spans):
                att_ref[:, s] = accum[g * rows : (g + 1) * rows] * keep_ref[:, s]

    count = 1
    while count <= chunks:
        low, high = count // 2, count
        pl.when((place >= low) & (place < high))(functools.partial(work, count))
        count *= 2
    done_ref[...] = jnp.zeros_like(done_ref)


def mix_head(group, first, att_ref, sh_ref, sl_ref, mult_ref, memory_ref):
    rows = att_ref.shape[0]
    m_hi, m_lo = split(memory_ref[...])
    spans = [pl.ds(pl.multiple_of((first + g) * HD, HD), HD) for g in range(group)]
    f_hi = jnp.concatenate([sh_ref[:, s] for s in spans], 0)
    f_lo = jnp.concatenate([sl_ref[:, s] for s in spans], 0)
    r = dot(jnp.concatenate([f_hi, f_lo], 1), jnp.concatenate([m_hi, m_hi], 0), ((1,), (0,)))
    r = r + dot(f_hi, m_lo, ((1,), (0,)))
    r = r * lax.rsqrt(jnp.mean(r * r, axis=1, keepdims=True) + EPS)
    return [
        (s, att_ref[:, s] + r[g * rows : (g + 1) * rows] * mult_ref[:, s])
        for g, s in enumerate(spans)
    ]


def own_mix_kernel(group, lines, *refs):
    for g, (_, mixed) in enumerate(mix_head(group, carried_head(lines) * group, *refs[:5])):
        refs[5][g] = mixed


def final_kernel(group, lines, *refs):
    ready_ref, out_ref, tile_ref, sems = refs[5:]
    own = carried_head(lines)
    copies = []
    for g in range(group):
        s = pl.ds(pl.multiple_of((own * group + g) * HD, HD), HD)
        copies.append(pltpu.make_async_copy(ready_ref.at[g], out_ref.at[:, s], sems.at[g]))
        copies[-1].start()
    for g, (s, mixed) in enumerate(mix_head(group, (1 - own) * group, *refs[:5])):
        tile_ref[g] = mixed
        copies.append(pltpu.make_async_copy(tile_ref.at[g], out_ref.at[:, s], sems.at[group + g]))
        copies[-1].start()
    for copy in copies:
        copy.wait()


def solution(mesh):
    n_seg, n_blk = mesh.shape["seg"], mesh.shape["blk"]
    both = ("seg", "blk")

    def swap(x, seg_bits, blk_bits):
        pairs = [
            (s * n_blk + b, (s ^ seg_bits) * n_blk + (b ^ blk_bits))
            for s in range(n_seg)
            for b in range(n_blk)
        ]
        return lax.ppermute(x, both, pairs)

    bits = [("seg", i) for i in reversed(range(n_seg.bit_length() - 1))]
    bits += [("blk", i) for i in reversed(range(1, n_blk.bit_length() - 1))]
    groups = [bits[i : i + 2] for i in range(0, len(bits), 2)]
    flips = dict(zip(groups[0], (0, 0), strict=False))
    flips.update(zip(groups[-1], (0, 1), strict=False))
    lines = [line for line in bits if flips.get(line)]

    def masks_of(number):
        found = [(0, 0)]
        for axis, bit in reversed(groups[number]):
            flip = flips.get((axis, bit), 0)
            step = (1 << bit, flip) if axis == "seg" else (0, (1 << bit) ^ flip)
            found += [(s ^ step[0], b ^ step[1]) for s, b in found]
        return [found[i] for i in ((3, 1, 2) if number == 0 and len(found) > 3 else (3, 2, 1) if len(found) == 4 else range(1, len(found)))]

    def on_device(queries, keys, values, gate_logit, memory_gain):
        rows, width = queries.shape
        group = width // keys.shape[1]
        square = jax.ShapeDtypeStruct((HD, HD), jnp.float32)

        def pass_on(kernel, inputs, loose, passed, outs, flops, passing=pl.BlockSpec(memory_space=pl.ANY)):
            anywhere = pl.BlockSpec(memory_space=pl.ANY)
            count, n_out = len(inputs) + len(loose), len(outs)
            return pl.pallas_call(
                kernel,
                in_specs=[pl.BlockSpec()] * len(inputs) + [anywhere] * len(loose) + [passing] * len(passed),
                out_specs=[pl.BlockSpec()] * n_out + [passing] * len(passed),
                out_shape=outs
                + [jax.ShapeDtypeStruct(x.shape, x.dtype) for x in passed],
                input_output_aliases={count + i: n_out + i for i in range(len(passed))},
                compiler_params=pltpu.CompilerParams(vmem_limit_bytes=8 * 1024 * 1024),
                cost_estimate=pl.CostEstimate(
                    flops=flops, bytes_accessed=500_000, transcendentals=20_000
                ),
            )(*inputs, *loose, *passed)

        k_core, v_core = swap(keys, 0, 1), swap(values, 0, 1)
        own = jnp.concatenate([keys, values], 1)
        part, own = pass_on(
            functools.partial(chip_kernel, lines), [k_core, v_core], [], [own], [square], 500_000_000, pl.BlockSpec()
        )
        gate, gain = gate_logit.reshape(1, -1), memory_gain.reshape(1, -1)
        wide = jax.ShapeDtypeStruct((rows, width), jnp.float32)
        half = jax.ShapeDtypeStruct((rows, width), jnp.bfloat16)
        line = jax.ShapeDtypeStruct((1, width), jnp.float32)
        large = pltpu.CompilerParams(vmem_limit_bytes=24 * 1024 * 1024)
        q_hi, q_lo, f_hi, f_lo, mult, keep = pl.pallas_call(
            functools.partial(prepare_kernel, group),
            out_shape=(half, half, half, half, line, line),
            compiler_params=large,
            cost_estimate=pl.CostEstimate(
                flops=1_000_000, bytes_accessed=100_000, transcendentals=0
            ),
        )(queries, gate, gain)

        held = [own, None]
        fresh = [swap(own, 0, 3)] if n_blk > 2 else []

        carried = None
        sends = {s: part for s, _ in masks_of(0)}
        for number in range(len(groups)):
            masks = masks_of(number)
            got = [swap(sends[s], s, b) for s, b in masks]
            last = number == len(groups) - 1
            nexts = [] if last else sorted({s for s, _ in masks_of(number + 1) if s})
            some = [] if carried is None else [carried]
            loose = [mult] if number == 0 else [done] if last else []
            carried, *extra = pass_on(
                functools.partial(combine_kernel, masks, nexts, len(some), len(loose)),
                [part, *got, *some],
                loose,
                [],
                [square] * (1 + len(nexts)),
                10_000_000_000 if number == 0 else 100_000,
            )
            sends = {0: carried, **dict(zip(nexts, extra, strict=True))}
            if number == 0:
                step = 2
                while step < n_blk:
                    news = fresh if step == 2 else [swap(held[m], 0, step) for m in range(0, step, 2)]
                    for new in news:
                        near = swap(new, 0, 1)
                        held += [near, new] if step == 2 else [new, near]
                    step *= 2
                att, done = pl.pallas_call(
                    functools.partial(attention_kernel, group, n_blk),
                    out_shape=(wide, jax.ShapeDtypeStruct((8, HD), jnp.float32)),
                    compiler_params=large,
                    cost_estimate=pl.CostEstimate(
                        flops=1_000_000, bytes_accessed=100_000, transcendentals=0
                    ),
                )(q_hi, q_lo, k_core, v_core, own, *held[2:], keep)
        other = swap(carried, 0, 1)

        tiles = (group, rows, HD)
        small = pltpu.CompilerParams(vmem_limit_bytes=16 * 1024 * 1024)
        ready = pl.pallas_call(
            functools.partial(own_mix_kernel, group, lines),
            out_shape=jax.ShapeDtypeStruct(tiles, jnp.float32),
            compiler_params=small,
            cost_estimate=pl.CostEstimate(
                flops=1_000_000_000, bytes_accessed=500_000, transcendentals=0
            ),
        )(att, f_hi, f_lo, mult, carried)
        return pl.pallas_call(
            functools.partial(final_kernel, group, lines),
            out_specs=pl.BlockSpec(memory_space=pl.ANY),
            out_shape=wide,
            scratch_shapes=[
                pltpu.VMEM(tiles, jnp.float32),
                pltpu.SemaphoreType.DMA((2 * group,)),
            ],
            compiler_params=small,
        )(att, f_hi, f_lo, mult, other, ready)

    return jax.shard_map(
        on_device,
        mesh=mesh,
        in_specs=(P(both, None), P(both, None), P(both, None), P(), P()),
        out_specs=P(both, None),
        check_vma=False,
    )
```
